32 devices in a mesh: group: 2 (over x), tensor: 8 (over z, y), side: 2 (over core).
Axes of the slice: x: 2, y: 2, z: 4, core: 2. Of those that a mesh axis runs over, the one named last changes fastest.
Arguments:
- hidden_pre: bfloat16 [32, 64, 4096], P('group', None, ('tensor', 'side')), parts along dimension 0, may hold values from -6 to 6
- coeff_pre: bfloat16 [32, 64, 2048], P(('group', 'tensor', 'side')), parts along dimension 0, may hold values from -6 to 6
- gate_pre: bfloat16 [32, 64, 4096], P('group', None, ('tensor', 'side')), parts along dimension 0, may hold values from -6 to 6
- step_raw: float32 [64, 32, 64], P(('tensor', 'side'), 'group'), parts along dimension 1, may hold values from -6 to 6
- cache_rows: bfloat16 [32, 64, 2048], P('group', ('tensor', 'side')), parts along dimension 0, may hold values from -6 to 6
- lengths: int32 [32], P('group'), parts along dimension 0, may hold values from 1 to 64, 512 in all
- owners: int32 [32, 1], P('group'), parts along dimension 0, may hold values from 0 to 15, as said below
- page_table: int32 [32, 8], P(('group', 'tensor', 'side')), parts along dimension 0, may hold values from 0 to 7, each once within a row
- conv_hidden: bfloat16 [4, 4096], replicated, may hold values from -3 to 3
- conv_coeff: bfloat16 [4, 2048], replicated, may hold values from -3 to 3
- step_bias: float32 [64], replicated, may hold values from -2 to 0
- decay_log: float32 [64], replicated, may hold values from -6.5 to -2
- skip_gain: float32 [64], replicated, may hold values from 0.5 to 1.5
- norm_gain: float32 [4096], replicated, may hold values from 0.5 to 1.5
- new_hidden: bfloat16 [64, 2, 4096], P(('group', 'tensor', 'side')), parts along dimension 0, may hold values from -6 to 6
- new_coeff: bfloat16 [64, 2, 2048], P(('group', 'tensor', 'side')), parts along dimension 0, may hold values from -6 to 6
- new_gate: bfloat16 [64, 2, 4096], P(('group', 'tensor', 'side')), parts along dimension 0, may hold values from -6 to 6
- new_step: float32 [64, 2, 64], P(('group', 'tensor', 'side')), parts along dimension 0, may hold values from -6 to 6
- new_query: bfloat16 [64, 2, 8192], P(('group', 'tensor', 'side')), parts along dimension 0, may hold values from -6 to 6
- new_cache: bfloat16 [64, 2, 2048], P(('group', 'tensor', 'side')), parts along dimension 0, may hold values from -6 to 6
Outputs:
- prefill_out: bfloat16 [32, 64, 4096], P('group', None, ('tensor', 'side')), parts along dimension 0
- cache_pool: bfloat16 [256, 16, 2048], P(('group', 'tensor', 'side')), parts along dimension 0
- decode_mixer: bfloat16 [64, 2, 4096], P(('group', 'tensor', 'side')), parts along dimension 0
- decode_attention: bfloat16 [64, 2, 8192], P(('group', 'tensor', 'side')), parts along dimension 0
The draws below stay inside these ranges and needn't reach their ends.
There are 2 independent parts, one for each index of `group`. The reference program is written for one: setup_inputs(seed, part) draws one part's arguments, and reference() takes and returns one part's arrays. A program takes and returns all parts, laid end to end along the dimension named above; an argument that names none is the same for every part. Nothing has to cross between parts.
Inputs may be any that keep to these rules, and one draw needn't show every extreme that they name: `lengths`: they add up to 512; the longest prompt has exactly 64 positions. 4 owners get two prompts, 8 owners get one, the others none. `page_table`: each row is a permutation of the owner's pages.
All inputs are finite; a program needn't handle non-finite values.
Results may differ from the reference program's by a relative error of at most 0.0054.
Values may be sent and summed in bfloat16 or wider, within the bound.
No kernel may reach another device: no remote copies, remote signals or barrier semaphores. Data moves between devices by JAX's collectives and lax.ppermute only.
A program may use at most 128 MiB of HBM per device.

```python
import math
import jax
import jax.numpy as jnp
import numpy as np
from jax import lax

HD = 64
NS = 128
GROUPS = 8
CONVK = 4
KVH = 8
KVD = 128
QH = 64
SPAN = 64
BLK = 16
SLOTS = 2
STEPS = 2
DEVS = 16
REQ = 16
HEADS = 64
NB = 4
POOL = 8


def draw_owners(key, part):
    key = jax.random.fold_in(key, 11)
    first_key, second_key = jax.random.split(key)
    owner_order = jax.random.permutation(first_key, REQ)
    request_ids = jnp.arange(REQ)
    picked = jnp.where(request_ids < REQ // 2, request_ids // 2, request_ids - REQ // 4)
    base_owner = owner_order[picked]
    shuffle = jax.random.permutation(second_key, REQ)
    return base_owner[shuffle].reshape(REQ, 1).astype(jnp.int32)


def draw_cache_rows(key, part):
    key = jax.random.fold_in(key, 5)
    array_shape = (REQ, SPAN, 2 * KVH * KVD)
    return jnp.clip(jax.random.normal(key, array_shape, jnp.float32), -6.0, 6.0).astype(jnp.bfloat16)


def draw_new_query(key, part):
    key = jax.random.fold_in(key, 6)
    array_shape = (DEVS * SLOTS, STEPS, QH * KVD)
    return jnp.clip(jax.random.normal(key, array_shape, jnp.float32), -6.0, 6.0).astype(jnp.bfloat16)


def levels(rng, dims, pieces, least, largest):
    factor_of, own = 1.0, jax.random.fold_in(rng, 6)
    for position, parts in pieces:
        draws = jnp.exp(jax.random.uniform(jax.random.fold_in(own, position), (parts,), jnp.float32, least / len(pieces), largest / len(pieces)))
        factor_of = factor_of * jnp.repeat(draws, dims[position] // parts).reshape([-1 if axis == position else 1 for axis in range(len(dims))])
    return factor_of


def length_profile(amount, total, bound, lean):
    portions = [(1 << 20) // math.isqrt(grade ** lean) + 1 for grade in range(2, amount + 1)]
    spare, given = total - bound - (amount - 1), [1] * (amount - 1)
    while spare > 0:
        candidates = [i for i in range(amount - 1) if given[i] < bound]
        pool, budget = sum([portions[i] for i in candidates]), spare
        for i in candidates:
            extra = min(bound - given[i], max(1, budget * portions[i] // pool), spare)
            given[i] = given[i] + extra
            spare = spare - extra
    return np.array([bound] + given)


def ragged_sizes(own_key, amount, total, limit, lean):
    if amount == 2:
        one = jax.random.randint(own_key, (), max(1, total - limit), min(limit, total - 1) + 1)
        return jnp.stack([one, total - one])
    tallies = jnp.asarray(length_profile(amount, total, limit, lean), jnp.int32)
    couples = (amount - 1) // 2
    giver, receiver = tallies[1:1 + 2 * couples:2], tallies[2:2 + 2 * couples:2]
    margin = jnp.minimum(giver - 1, limit - receiver)
    shifted = jax.random.randint(jax.random.fold_in(own_key, 1), (couples,), 0, 1 << 20) % (margin + 1)
    tallies = tallies.at[1:1 + 2 * couples:2].set(giver - shifted).at[2:2 + 2 * couples:2].set(receiver + shifted)
    return tallies[jax.random.permutation(jax.random.fold_in(own_key, 2), amount)]


def normal_values(own_key, shape, deviation, reach, shards=(), held_as=jnp.bfloat16):
    array = deviation * jax.random.normal(own_key, shape, jnp.float32)
    if shards:
        array = array * levels(own_key, shape, shards, -0.22, 0.18)
    return jnp.clip(array, -reach, reach).astype(held_as)


def setup_inputs(seed: int = 0, part: int = 0) -> dict:
    keys = jax.random.split(jax.random.key(seed), 21)
    part_keys = jax.random.split(jax.random.fold_in(keys[20], part), 21)
    return {
        "hidden_pre": normal_values(part_keys[0], (REQ, SPAN, HEADS * HD), 1.0, 6.0, ((2, 16),)),
        "coeff_pre": normal_values(part_keys[1], (REQ, SPAN, GROUPS * 2 * NS), 1.0, 6.0, ((0, 16),)),
        "gate_pre": normal_values(part_keys[2], (REQ, SPAN, HEADS * HD), 1.0, 6.0, ((2, 16),)),
        "step_raw": normal_values(part_keys[3], (HEADS, REQ, SPAN), 1.0, 6.0, ((0, 16),), jnp.float32),
        "cache_rows": draw_cache_rows(jax.random.fold_in(jax.random.fold_in(keys[20], part), 71), part),
        "lengths": ragged_sizes(part_keys[5], REQ, REQ * SPAN // 2, SPAN, 2).astype(jnp.int32),
        "owners": draw_owners(jax.random.fold_in(jax.random.fold_in(keys[20], part), 71), part),
        "page_table": jax.vmap(lambda own: jax.random.permutation(own, POOL))(jax.random.split(part_keys[7], DEVS)).reshape((DEVS, POOL)).astype(jnp.int32),
        "conv_hidden": normal_values(keys[8], (CONVK, HEADS * HD), CONVK ** -0.5, 3.0),
        "conv_coeff": normal_values(keys[9], (CONVK, GROUPS * 2 * NS), CONVK ** -0.5, 3.0),
        "step_bias": jnp.clip(jax.random.uniform(keys[10], (HEADS,), jnp.float32, -2.0, 0.0), -2.0, 0.0),
        "decay_log": jnp.clip(jax.random.uniform(keys[11], (HEADS,), jnp.float32, -6.5, -2.0), -6.5, -2.0),
        "skip_gain": jnp.clip(jax.random.uniform(keys[12], (HEADS,), jnp.float32, 0.5, 1.5), 0.5, 1.5),
        "norm_gain": jnp.clip(1.0 + 0.1 * jax.random.normal(keys[13], (HEADS * HD,), jnp.float32), 0.5, 1.5),
        "new_hidden": normal_values(part_keys[14], (DEVS * SLOTS, STEPS, HEADS * HD), 1.0, 6.0, ((0, 16),)),
        "new_coeff": normal_values(part_keys[15], (DEVS * SLOTS, STEPS, GROUPS * 2 * NS), 1.0, 6.0, ((0, 16),)),
        "new_gate": normal_values(part_keys[16], (DEVS * SLOTS, STEPS, HEADS * HD), 1.0, 6.0, ((0, 16),)),
        "new_step": normal_values(part_keys[17], (DEVS * SLOTS, STEPS, HEADS), 1.0, 6.0, ((0, 16),), jnp.float32),
        "new_query": draw_new_query(jax.random.fold_in(jax.random.fold_in(keys[20], part), 71), part),
        "new_cache": normal_values(part_keys[19], (DEVS * SLOTS, STEPS, 2 * KVH * KVD), 1.0, 6.0, ((0, 16),)),
    }


epsilon = 1e-05

def causal_conv(padded, weight):
    row_count = padded.shape[-2] - weight.shape[0] + 1
    running = jnp.zeros(padded.shape[:-2] + (row_count, padded.shape[-1]), jnp.float32)
    for tap_index in range(weight.shape[0]):
        running = running + padded[..., tap_index:tap_index + row_count, :] * weight[tap_index]
    return jax.nn.silu(running).astype(jnp.bfloat16)

def gated_norm(output_rows, gate_values, norm_gain):
    gated = output_rows * jax.nn.silu(gate_values.astype(jnp.float32))
    row_scale = lax.rsqrt(lax.optimization_barrier(jnp.mean(gated * gated, axis=-1, keepdims=True)) + epsilon)
    return gated * row_scale * norm_gain

def reference(hidden_pre, coeff_pre, gate_pre, step_raw, cache_rows, lengths, owners, page_table, conv_hidden, conv_coeff, step_bias, decay_log, skip_gain, norm_gain, new_hidden, new_coeff, new_gate, new_step, new_query, new_cache):
    highest = lax.Precision.HIGHEST
    heads = decay_log.shape[0]
    width = heads * HD
    per_group = heads // GROUPS
    decay_rate = -jnp.exp(decay_log)
    weight_hidden = conv_hidden.astype(jnp.float32)
    weight_coeff = conv_coeff.astype(jnp.float32)
    positions = jnp.arange(SPAN)
    lower = positions[:, None] >= positions[None, :]
    hidden_padded = jnp.pad(hidden_pre, ((0, 0), (CONVK - 1, 0), (0, 0)))
    coeff_padded = jnp.pad(coeff_pre, ((0, 0), (CONVK - 1, 0), (0, 0)))

    def prefill_one(request_id):
        length = lengths[request_id]
        is_valid = positions < length
        hidden_conv = causal_conv(hidden_padded[request_id].astype(jnp.float32), weight_hidden).reshape(SPAN, heads, HD)
        coeff_conv = causal_conv(coeff_padded[request_id].astype(jnp.float32), weight_coeff).reshape(SPAN, GROUPS, 2, NS)
        b_group = coeff_conv[:, :, 0, :].astype(jnp.float32)
        c_group = coeff_conv[:, :, 1, :].astype(jnp.float32)
        step_size = jax.nn.softplus(step_raw[:, request_id, :].T + step_bias) * is_valid[:, None]
        cumulative = jnp.cumsum(step_size * decay_rate, axis=0)
        group_scores = jnp.einsum('tgn,sgn->gts', c_group, b_group, precision=highest)
        head_scores = jnp.repeat(group_scores, per_group, axis=0)
        difference = cumulative.T[:, :, None] - cumulative.T[:, None, :]
        segment = jnp.exp(jnp.where(lower[None], difference, -jnp.inf))
        mixing = (head_scores * segment * step_size.T[:, None, :]).astype(jnp.bfloat16)
        hidden_float = hidden_conv.astype(jnp.float32)
        output_heads = jnp.einsum('hts,shd->thd', mixing.astype(jnp.float32), hidden_float, precision=highest) + skip_gain[None, :, None] * hidden_float
        end_weight = jnp.exp(cumulative[-1] - cumulative) * step_size
        weighted = (hidden_float * end_weight[:, :, None]).astype(jnp.bfloat16)
        b_heads = jnp.repeat(b_group, per_group, axis=1)
        ssm_state = jnp.einsum('shd,shn->hdn', weighted.astype(jnp.float32), b_heads, precision=highest).astype(jnp.bfloat16)
        normed = gated_norm(output_heads.reshape(SPAN, width), gate_pre[request_id], norm_gain)
        prefill_row = (normed * is_valid[:, None]).astype(jnp.bfloat16)
        tail_hidden = lax.dynamic_slice_in_dim(hidden_padded[request_id], length.astype(jnp.int32), CONVK - 1, 0)
        tail_coeff = lax.dynamic_slice_in_dim(coeff_padded[request_id], length.astype(jnp.int32), CONVK - 1, 0)
        return (prefill_row, ssm_state, tail_hidden, tail_coeff)
    prefill_out, states, tails_hidden, tails_coeff = lax.map(prefill_one, jnp.arange(REQ, dtype=jnp.int32))
    owner_id = owners[:, 0]
    request_ids = jnp.arange(REQ, dtype=jnp.int32)
    same_owner = (owner_id[:, None] == owner_id[None, :]) & (request_ids[None, :] < request_ids[:, None])
    slot_rank = lax.optimization_barrier(jnp.sum(same_owner.astype(jnp.int32), axis=1))
    target = owner_id * SLOTS + slot_rank
    slot_total = DEVS * SLOTS
    filled = jnp.zeros((slot_total,), jnp.float32).at[target].set(1.0)
    slot_length = jnp.zeros((slot_total,), jnp.int32).at[target].set(lengths)
    slot_state = jnp.zeros((slot_total, heads, HD, NS), jnp.bfloat16).at[target].set(states)
    slot_tail_hidden = jnp.zeros((slot_total, CONVK - 1, width), jnp.bfloat16).at[target].set(tails_hidden)
    slot_tail_coeff = jnp.zeros((slot_total, CONVK - 1, GROUPS * 2 * NS), jnp.bfloat16).at[target].set(tails_coeff)
    live_rows = positions[None, :] < lengths[:, None]
    cache_kept = jnp.where(live_rows[:, :, None], cache_rows, jnp.zeros((), jnp.bfloat16))
    slot_cache = jnp.zeros((slot_total, SPAN, 2 * KVH * KVD), jnp.bfloat16).at[target].set(cache_kept)
    blocks = slot_cache.reshape(slot_total * NB, BLK, 2 * KVH * KVD)
    page_dest = (jnp.arange(DEVS, dtype=jnp.int32)[:, None] * POOL + page_table).reshape(-1)
    cache_pool = jnp.zeros((DEVS * POOL, BLK, 2 * KVH * KVD), jnp.bfloat16).at[page_dest].set(blocks)
    query_scale = KVD ** (-0.5)
    places = jnp.arange(SPAN + STEPS)
    step_ids = jnp.arange(STEPS)

    def decode_one(slot_id):
        ssm_state = slot_state[slot_id].astype(jnp.float32)
        slot_fill = filled[slot_id]
        hidden_rows = jnp.concatenate([slot_tail_hidden[slot_id], new_hidden[slot_id]], axis=0).astype(jnp.float32)
        coeff_rows = jnp.concatenate([slot_tail_coeff[slot_id], new_coeff[slot_id]], axis=0).astype(jnp.float32)
        hidden_conv = causal_conv(hidden_rows, weight_hidden)
        coeff_conv = causal_conv(coeff_rows, weight_coeff).reshape(STEPS, GROUPS, 2, NS)
        mixer_rows = []
        for step_index in range(STEPS):
            step_size = jax.nn.softplus(new_step[slot_id, step_index] + step_bias)
            hidden_now = hidden_conv[step_index].reshape(heads, HD).astype(jnp.float32)
            b_now = jnp.repeat(coeff_conv[step_index, :, 0, :], per_group, axis=0).astype(jnp.float32)
            c_now = jnp.repeat(coeff_conv[step_index, :, 1, :], per_group, axis=0).astype(jnp.float32)
            ssm_state = jnp.exp(step_size * decay_rate)[:, None, None] * ssm_state + (step_size[:, None] * hidden_now)[:, :, None] * b_now[:, None, :]
            readout = lax.optimization_barrier(jnp.sum(ssm_state * c_now[:, None, :], axis=-1)) + skip_gain[:, None] * hidden_now
            normed = gated_norm(readout.reshape(width), new_gate[slot_id, step_index], norm_gain)
            mixer_rows.append((normed * slot_fill).astype(jnp.bfloat16))
        cache_all = jnp.concatenate([slot_cache[slot_id], new_cache[slot_id]], axis=0)
        key_part = cache_all[:, :KVH * KVD].reshape(SPAN + STEPS, KVH, KVD).astype(jnp.float32)
        value_part = cache_all[:, KVH * KVD:].reshape(SPAN + STEPS, KVH, KVD).astype(jnp.float32)
        query_heads = new_query[slot_id].reshape(STEPS, KVH, QH // KVH, KVD).astype(jnp.float32)
        logits = jnp.einsum('qkgd,jkd->qkgj', query_heads, key_part, precision=highest) * query_scale
        is_live = (places[None, :] < slot_length[slot_id]) | (places[None, :] >= SPAN) & (places[None, :] - SPAN <= step_ids[:, None])
        is_live = is_live[:, None, None, :]
        row_peak = lax.optimization_barrier(jnp.max(jnp.where(is_live, logits, -jnp.inf), axis=-1, keepdims=True))
        exponent = jnp.exp(jnp.where(is_live, logits - row_peak, -jnp.inf))
        softmax_weights = (exponent / lax.optimization_barrier(jnp.sum(exponent, axis=-1, keepdims=True))).astype(jnp.bfloat16)
        attended = jnp.einsum('qkgj,jkd->qkgd', softmax_weights.astype(jnp.float32), value_part, precision=highest)
        attention_row = (attended.reshape(STEPS, QH * KVD) * slot_fill).astype(jnp.bfloat16)
        return (jnp.stack(mixer_rows, axis=0), attention_row)
    decode_mixer, decode_attention = lax.map(decode_one, jnp.arange(slot_total, dtype=jnp.int32))
    return (prefill_out, cache_pool, decode_mixer, decode_attention)
```

```python
import jax
import jax.numpy as jnp
from jax import lax
from jax.experimental import pallas as pl
from jax.experimental.pallas import tpu as pltpu
from jax.sharding import PartitionSpec as P

GROUPS = 8
CONVK = 4
KVH = 8
KVD = 128
BLK = 16
LANES = 128
ROWS = 80
NEW = 16
EPS = 1e-05
AXES = ("tensor", "side")
F32 = jnp.float32
BF16 = jnp.bfloat16

SMEM = pl.BlockSpec(memory_space=pltpu.SMEM)
VMEM = pl.BlockSpec(memory_space=pltpu.VMEM)
PARAMS = pltpu.CompilerParams(vmem_limit_bytes=48 * 1024 * 1024)


def iota(shape, dim):
    return lax.broadcasted_iota(jnp.int32, shape, dim)


def softplus(x):
    return jnp.maximum(x, 0.0) + jnp.log1p(jnp.exp(-jnp.abs(x)))


def silu(x):
    return x / (1.0 + jnp.exp(-x))


def ranks(owners, count, rank_ref):
    def clear(d, carry):
        count[d] = 0
        return carry

    lax.fori_loop(0, count.shape[0], clear, 0)

    def one(r, carry):
        owner = owners[r, 0]
        rank = count[owner]
        rank_ref[r] = rank
        count[owner] = rank + 1
        return carry

    lax.fori_loop(0, owners.shape[0], one, 0)


def pack_kernel(owners, coeff, cache, hidden, coeff_new, step_new, send, count, source):
    devices = send.shape[0]
    slots = hidden.shape[0]
    group_devs = devices // GROUPS
    span = coeff.shape[1]
    width = cache.shape[2]

    def clear(d, carry):
        count[d] = 0
        for k in range(slots):
            source[d * slots + k] = 0
        return carry

    lax.fori_loop(0, devices, clear, 0)

    def place(r, carry):
        owner = owners[r, 0]
        rank = count[owner]
        source[owner * slots + rank] = r
        count[owner] = rank + 1
        return carry

    lax.fori_loop(0, owners.shape[0], place, 0)

    heads = step_new.shape[2]
    steps = jnp.concatenate([step_new[k] for k in range(slots)], axis=0)
    if heads < LANES:
        steps = jnp.concatenate(
            [steps, jnp.zeros((steps.shape[0], LANES - heads), F32)], axis=1
        )
    steps = jnp.concatenate([steps, jnp.zeros_like(steps)], axis=0)
    padded = steps.shape[1]
    lane = iota((8, LANES), 1)

    def one(d, carry):
        group = d // group_devs
        start = pl.multiple_of((group * 2 + lax.rem(d, 2)) * LANES, LANES)
        send[d, 0:span, :] = coeff[0, :, pl.ds(start, LANES)]
        own = pl.multiple_of(d * 2 * LANES, 2 * LANES)
        rows = jnp.concatenate(
            [hidden[k, :, pl.ds(own, 2 * LANES)].astype(F32) for k in range(slots)], axis=0
        )
        tokens = jnp.concatenate(
            [coeff_new[k, :, pl.ds(start, LANES)].astype(F32) for k in range(slots)], axis=0
        )
        mine = pltpu.roll(steps, lax.rem(padded - d * 4, padded), 1)[:, :LANES]
        high = mine.astype(BF16).astype(F32)
        rest = mine - high
        middle = rest.astype(BF16).astype(F32)
        low = rest - middle
        split = jnp.where(
            lane < 32, high, jnp.where(lane < 64, pltpu.roll(middle, 32, 1), pltpu.roll(low, 64, 1))
        )
        block = jnp.concatenate([rows[:, :LANES], rows[:, LANES:], tokens, split[0:4]], axis=0)
        send[d, span : span + NEW, :] = block.astype(BF16)
        kept = jnp.concatenate(
            [cache[source[d * slots + k]].astype(F32) for k in range(slots)], axis=0
        )
        kept = jnp.concatenate(
            [kept[:, c * LANES : (c + 1) * LANES] for c in range(width // LANES)], axis=0
        )
        send[d, span + NEW :, :] = kept.astype(BF16)
        return carry

    lax.fori_loop(0, devices, one, 0)


def spliced(rows, first, second, length):
    columns = rows.shape[1]
    rows = jnp.concatenate([rows, jnp.zeros((ROWS - rows.shape[0], columns), F32)], axis=0)
    place = iota((ROWS, columns), 0)
    return jnp.where(place == length, first, jnp.where(place == length + 1, second, rows))


def conv(rows, taps):
    total = pltpu.roll(rows, 3, 0) * taps[0:1]
    total = total + pltpu.roll(rows, 2, 0) * taps[1:2]
    total = total + pltpu.roll(rows, 1, 0) * taps[2:3]
    total = total + rows * taps[3:4]
    return silu(total).astype(BF16)


def coeff_kernel(owners, lengths, taps_ref, recv, out, count, rank_ref):
    prompts = out.shape[0]
    span = recv.shape[1] - NEW
    devices = recv.shape[0]
    group_devs = devices // GROUPS
    ranks(owners, count, rank_ref)
    me = lax.axis_index(AXES)
    start = pl.multiple_of((me // group_devs * 2 + lax.rem(me, 2)) * LANES, LANES)
    taps = taps_ref[:, pl.ds(start, LANES)].astype(F32)

    def one(r, carry):
        new = recv[owners[r, 0], span : span + NEW, :].astype(F32)
        is_first = rank_ref[r] == 0
        first = jnp.where(is_first, new[8:9], new[10:11])
        second = jnp.where(is_first, new[9:10], new[11:12])
        rows = spliced(recv[r, 0:span, :].astype(F32), first, second, lengths[r])
        out[r] = conv(rows, taps)
        return carry

    lax.fori_loop(0, prompts, one, 0, unroll=2)


def main_kernel(
    owners,
    lengths,
    bias,
    decay,
    skip,
    taps_ref,
    mine,
    other,
    new_ref,
    hidden,
    gate,
    step,
    gated_ref,
    fin,
    count,
    rank_ref,
    tokens,
    dt_ref,
    sum_ref,
):
    prompts, span, columns = hidden.shape
    local_heads = step.shape[0]
    head_size = columns // local_heads
    ranks(owners, count, rank_ref)
    me = lax.axis_index(AXES)
    is_b = lax.rem(me, 2) == 0
    taps = taps_ref[:, pl.ds(pl.multiple_of(me * columns, LANES), columns)].astype(F32)
    fin[...] = jnp.zeros_like(fin)

    def fetch(r, carry):
        new = new_ref[owners[r, 0]].astype(F32)
        is_first = rank_ref[r] == 0
        tokens[0, pl.ds(r, 1), :] = jnp.where(is_first, new[12:13], new[14:15])
        tokens[1, pl.ds(r, 1), :] = jnp.where(is_first, new[13:14], new[15:16])
        return carry

    lax.fori_loop(0, prompts, fetch, 0)

    def widths(r, lens):
        return jnp.where(iota((prompts, LANES), 0) == r, lengths[r], lens)

    lens = lax.fori_loop(0, prompts, widths, jnp.zeros((prompts, LANES), jnp.int32))
    lane = iota((prompts, LANES), 1)
    news = []
    for i in range(2):
        raw = tokens[i]
        news.append(raw + pltpu.roll(raw, LANES - 32, 1) + pltpu.roll(raw, LANES - 64, 1))
    for h in range(local_heads):
        raw = jnp.concatenate([step[h], jnp.zeros((prompts, LANES - span), F32)], axis=1)
        raw = jnp.where(
            lane == lens,
            news[0][:, h : h + 1],
            jnp.where(lane == lens + 1, news[1][:, h : h + 1], raw),
        )
        size = jnp.where(lane < lens + 2, softplus(raw + bias[me * local_heads + h]), 0.0)
        rate = -jnp.exp(jnp.full((1, LANES), decay[me * local_heads + h], F32))
        total = size * rate
        shift = 1
        while shift < LANES:
            total = total + jnp.where(lane >= shift, pltpu.roll(total, shift, 1), 0.0)
            shift *= 2
        dt_ref[:, h, :] = size
        sum_ref[:, h, :] = total

    head_of = iota((1, columns), 1) // head_size
    gain = jnp.zeros((1, columns), F32)
    for h in range(local_heads):
        gain = jnp.where(head_of == h, skip[me * local_heads + h], gain)
    heads_wide = iota((ROWS, columns), 1) // head_size
    place = iota((ROWS, columns), 0)
    lower = iota((ROWS, ROWS), 0) >= iota((ROWS, ROWS), 1)
    column_of = iota((span, LANES), 1)

    def one(r, squares):
        owner = owners[r, 0]
        rank = rank_ref[r]
        length = lengths[r]
        new = new_ref[owner].astype(F32)
        is_first = rank == 0
        token = []
        for i in range(2):
            a = jnp.where(is_first, new[i : i + 1], new[2 + i : 3 + i])
            b = jnp.where(is_first, new[4 + i : 5 + i], new[6 + i : 7 + i])
            token.append(jnp.concatenate([a, b], axis=1))
        u = conv(spliced(hidden[r].astype(F32), token[0], token[1], length), taps)
        here, there = mine[r], other[r]
        b_rows = jnp.where(is_b, here, there)
        c_rows = jnp.where(is_b, there, here)
        scores = lax.dot_general(
            c_rows, b_rows, (((1,), (1,)), ((), ())), preferred_element_type=F32
        )
        sums = sum_ref[r]
        sizes = dt_ref[r]
        turned = sums.T
        out = gain * u.astype(F32)
        for h in range(local_heads):
            gap = turned[:ROWS, h : h + 1] - sums[h : h + 1, :ROWS]
            mix = jnp.where(lower, scores * jnp.exp(gap) * sizes[h : h + 1, :ROWS], 0.0)
            only = jnp.where(heads_wide == h, u, jnp.zeros((), BF16))
            out = out + jnp.dot(mix.astype(BF16), only, preferred_element_type=F32)
        for i in range(2):
            row = jnp.sum(jnp.where(place == length + i, out, 0.0), axis=0, keepdims=True)
            for half in range(2):
                fin[owner, pl.ds(prompts // 2 + 4 * half + 2 * rank + i, 1), :] = row[
                    :, half * LANES : (half + 1) * LANES
                ]
        gated = out[:span] * silu(gate[r].astype(F32))
        gated_ref[r] = gated
        square = jnp.sum(gated * gated, axis=1, keepdims=True)
        return jnp.where(column_of == r, square, squares)

    squares = lax.fori_loop(0, prompts, one, jnp.zeros((span, LANES), F32))
    turned = squares.T
    half = prompts // 2
    packed = jnp.concatenate([turned[0:half, :], turned[half:prompts, :]], axis=1)

    def spread(d, carry):
        fin[d, 0:half, :] = packed
        return carry

    lax.fori_loop(0, fin.shape[0], spread, 0)


def slot_facts(owners, lengths, slots):
    me = lax.axis_index(AXES)

    def one(r, found):
        is_mine = owners[r, 0] == me
        seen = found[-1]
        lens = [
            jnp.where(is_mine & (seen == k), lengths[r], found[k]) for k in range(slots)
        ]
        return (*lens, seen + is_mine.astype(jnp.int32))

    zero = jnp.int32(0)
    return lax.fori_loop(0, owners.shape[0], one, (zero,) * (slots + 1))[:slots]


def cache_kernel(owners, lengths, pages, recv, query, cache_new, pool, attended, rows_ref):
    slots = query.shape[0]
    steps = query.shape[1]
    sources = recv.shape[0]
    width = pool.shape[2]
    parts = width // LANES
    span = sources * (recv.shape[1] // parts) // slots
    offset = 0
    each = recv.shape[1] // parts
    local = each // slots
    lens = slot_facts(owners, lengths, slots)
    keys = sources * each
    row = iota((slots * span, keys), 0)
    key = iota((slots * span, keys), 1)
    slot_of = row // span
    at = lax.rem(row, span)
    wanted = at // local * each + slot_of * local + lax.rem(at, local)
    limit = jnp.where(slot_of == 0, lens[0], lens[1])
    order = jnp.where((key == wanted) & (at < limit), 1.0, 0.0).astype(BF16)
    ask = jnp.concatenate([query[k].astype(F32) for k in range(slots)], axis=0)
    fresh = jnp.concatenate([cache_new[k].astype(F32) for k in range(slots)], axis=0)
    fresh = jnp.concatenate([fresh, jnp.zeros_like(fresh)], axis=0)
    per = query.shape[2] // (KVH * KVD)
    pairs = slots * steps
    count = per * pairs
    ask_slot = lax.rem(iota((count, slots * span), 0), pairs) // steps
    ask_step = lax.rem(iota((count, slots * span), 0), steps)
    key_slot = iota((count, slots * span), 1) // span
    key_at = lax.rem(iota((count, slots * span), 1), span)
    live = (key_slot == ask_slot) & (key_at < jnp.where(ask_slot == 0, lens[0], lens[1]))
    new_row = iota((count, 2 * pairs), 0)
    new_key = iota((count, 2 * pairs), 1)
    new_live = (
        (new_key < pairs)
        & (new_key // steps == lax.rem(new_row, pairs) // steps)
        & (lax.rem(new_key, steps) <= lax.rem(new_row, steps))
    )
    out_slot = lax.rem(iota((count, KVD), 0), pairs) // steps
    filled = jnp.where(out_slot == 0, lens[0], lens[1]) > 0

    for c in range(parts):
        block = recv[:, offset + c * each : offset + (c + 1) * each, :].astype(F32)
        block = block.reshape(keys, LANES).astype(BF16)
        rows_ref[:, c * LANES : (c + 1) * LANES] = jnp.dot(
            order, block, preferred_element_type=F32
        ).astype(BF16)
    blocks = span // BLK
    for k in range(slots):
        for b in range(blocks):
            pool[pages[0, k * blocks + b]] = rows_ref[
                k * span + b * BLK : k * span + (b + 1) * BLK, :
            ]
    contract = (((1,), (1,)), ((), ()))
    answers = []
    for c in range(KVH):
        asked = jnp.concatenate(
            [ask[:, (c * per + g) * KVD : (c * per + g + 1) * KVD] for g in range(per)], axis=0
        ).astype(BF16)
        own = slice(c * KVD, (c + 1) * KVD)
        values = slice((KVH + c) * KVD, (KVH + c + 1) * KVD)
        old = lax.dot_general(asked, rows_ref[:, own], contract, preferred_element_type=F32)
        recent = lax.dot_general(
            asked, fresh[:, own].astype(BF16), contract, preferred_element_type=F32
        )
        old = jnp.where(live, old * KVD ** (-0.5), -jnp.inf)
        recent = jnp.where(new_live, recent * KVD ** (-0.5), -jnp.inf)
        peak = jnp.maximum(
            jnp.max(old, axis=1, keepdims=True), jnp.max(recent, axis=1, keepdims=True)
        )
        old = jnp.exp(old - peak)
        recent = jnp.exp(recent - peak)
        total = jnp.sum(old, axis=1, keepdims=True) + jnp.sum(recent, axis=1, keepdims=True)
        got = jnp.dot(
            (old / total).astype(BF16), rows_ref[:, values], preferred_element_type=F32
        ) + jnp.dot(
            (recent / total).astype(BF16),
            fresh[:, values].astype(BF16),
            preferred_element_type=F32,
        )
        got = jnp.where(filled, got, 0.0)
        answers += [got[g * pairs : (g + 1) * pairs] for g in range(per)]
    whole = jnp.concatenate(answers, axis=1)
    for k in range(slots):
        attended[k] = whole[k * steps : (k + 1) * steps].astype(BF16)


def final_kernel(owners, lengths, gain_ref, fin, gated, new_gate, prefill, mixer):
    prompts, span, columns = gated.shape
    slots = new_gate.shape[0]
    steps = new_gate.shape[1]
    sources = fin.shape[0]
    width = new_gate.shape[2]
    half = prompts // 2
    me = lax.axis_index(AXES)
    total = fin[0, 0:half, :]
    for s in range(1, sources):
        total = total + fin[s, 0:half, :]
    scale = lax.rsqrt(total / width + EPS).T
    gain = gain_ref[:, pl.ds(pl.multiple_of(me * columns, LANES), columns)]
    place = iota((span, columns), 0)
    for r in range(prompts):
        low = 0 if r < half else span
        column = scale[low : low + span, r % half : r % half + 1]
        rows = gated[r] * column * gain
        prefill[r] = jnp.where(place < lengths[r], rows, 0.0).astype(BF16)
    lens = slot_facts(owners, lengths, slots)
    read = jnp.concatenate(
        [
            fin[s, half + pairs : half + pairs + 4, :]
            for s in range(sources)
            for pairs in (0, 4)
        ],
        axis=1,
    )
    gates = jnp.concatenate([new_gate[k].astype(F32) for k in range(slots)], axis=0)
    out = read * silu(gates)
    mean = jnp.mean(out * out, axis=1, keepdims=True)
    out = out * lax.rsqrt(mean + EPS) * gain_ref[...]
    slot_of = iota(out.shape, 0) // steps
    out = jnp.where(jnp.where(slot_of == 0, lens[0], lens[1]) > 0, out, 0.0)
    for k in range(slots):
        mixer[k] = out[k * steps : (k + 1) * steps].astype(BF16)


def local(
    hidden_pre,
    coeff_pre,
    gate_pre,
    step_raw,
    cache_rows,
    lengths,
    owners,
    page_table,
    conv_hidden,
    conv_coeff,
    step_bias,
    decay_log,
    skip_gain,
    norm_gain,
    new_hidden,
    new_coeff,
    new_gate,
    new_step,
    new_query,
    new_cache,
):
    devices = lax.axis_size(AXES)
    prompts, span, columns = hidden_pre.shape
    slots = new_hidden.shape[0]
    local_heads = step_raw.shape[0]
    cache_width = cache_rows.shape[2]
    kept_rows = slots * cache_rows.shape[1] * cache_width // LANES
    per_owner = pltpu.SMEM((devices,), jnp.int32)
    per_prompt = pltpu.SMEM((prompts,), jnp.int32)

    send = pl.pallas_call(
        pack_kernel,
        out_shape=jax.ShapeDtypeStruct((devices, span + NEW + kept_rows, LANES), BF16),
        in_specs=[SMEM, VMEM, VMEM, VMEM, VMEM, VMEM],
        out_specs=VMEM,
        scratch_shapes=[per_owner, pltpu.SMEM((devices * slots,), jnp.int32)],
        compiler_params=PARAMS,
        name="pack",
    )(owners, coeff_pre, cache_rows, new_hidden, new_coeff, new_step)
    recv = lax.all_to_all(send, AXES, split_axis=0, concat_axis=0, tiled=True)

    mine = pl.pallas_call(
        coeff_kernel,
        grid=(1,),
        out_shape=jax.ShapeDtypeStruct((prompts, ROWS, LANES), BF16),
        in_specs=[
            SMEM,
            SMEM,
            VMEM,
            pl.BlockSpec((devices, span + NEW, LANES), lambda i: (0, 0, 0)),
        ],
        out_specs=VMEM,
        scratch_shapes=[per_owner, per_prompt],
        compiler_params=PARAMS,
        name="coeff",
    )(owners, lengths, conv_coeff, recv)
    other = lax.ppermute(mine, "side", [(0, 1), (1, 0)])

    new_block = span // NEW
    gated, fin = pl.pallas_call(
        main_kernel,
        grid=(1,),
        out_shape=(
            jax.ShapeDtypeStruct((prompts, span, columns), F32),
            jax.ShapeDtypeStruct((devices, prompts // 2 + 8, LANES), F32),
        ),
        in_specs=[SMEM] * 5
        + [VMEM] * 3
        + [pl.BlockSpec((devices, NEW, LANES), lambda i: (0, new_block, 0))]
        + [VMEM] * 3,
        out_specs=(VMEM, VMEM),
        scratch_shapes=[
            per_owner,
            per_prompt,
            pltpu.VMEM((2, prompts, LANES), F32),
            pltpu.VMEM((prompts, 8, LANES), F32),
            pltpu.VMEM((prompts, 8, LANES), F32),
        ],
        compiler_params=PARAMS,
        name="main",
    )(
        owners,
        lengths,
        step_bias,
        decay_log,
        skip_gain,
        conv_hidden,
        mine,
        other,
        recv,
        hidden_pre,
        gate_pre,
        step_raw,
    )
    fin_got = lax.all_to_all(fin, AXES, split_axis=0, concat_axis=0, tiled=True)

    kept = recv[:, span + NEW :, :]
    cache_pool, decode_attention = pl.pallas_call(
        cache_kernel,
        out_shape=(
            jax.ShapeDtypeStruct((page_table.shape[1], BLK, cache_width), BF16),
            jax.ShapeDtypeStruct(new_query.shape, BF16),
        ),
        in_specs=[SMEM, SMEM, SMEM, VMEM, VMEM, VMEM],
        out_specs=(VMEM, VMEM),
        scratch_shapes=[pltpu.VMEM((slots * span, cache_width), BF16)],
        compiler_params=PARAMS,
        cost_estimate=pl.CostEstimate(
            flops=200_000_000, bytes_accessed=4_000_000, transcendentals=100_000
        ),
        name="cache",
    )(owners, lengths, page_table, kept, new_query, new_cache)

    prefill_out, decode_mixer = pl.pallas_call(
        final_kernel,
        out_shape=(
            jax.ShapeDtypeStruct(hidden_pre.shape, BF16),
            jax.ShapeDtypeStruct(new_gate.shape, BF16),
        ),
        in_specs=[SMEM, SMEM, VMEM, VMEM, VMEM, VMEM],
        out_specs=(VMEM, VMEM),
        compiler_params=PARAMS,
        name="final",
    )(owners, lengths, norm_gain.reshape(1, -1), fin_got, gated, new_gate)
    return (prefill_out, cache_pool, decode_mixer, decode_attention)


def solution(mesh):
    own = P(("group", "tensor", "side"), None, None)
    placed = (
        P("group", None, ("tensor", "side")),
        own,
        P("group", None, ("tensor", "side")),
        P(("tensor", "side"), "group", None),
        P("group", ("tensor", "side"), None),
        P("group"),
        P("group", None),
        P(("group", "tensor", "side"), None),
        P(),
        P(),
        P(),
        P(),
        P(),
        P(),
        own,
        own,
        own,
        own,
        own,
        own,
    )
    return jax.shard_map(
        local,
        mesh=mesh,
        in_specs=placed,
        out_specs=(P("group", None, ("tensor", "side")), own, own, own),
        check_vma=False,
    )
```

```python
import jax
import jax.numpy as jnp
from jax import lax
from jax.experimental import pallas as pl
from jax.experimental.pallas import tpu as pltpu
from jax.sharding import PartitionSpec as P

GROUPS = 8
CONVK = 4
KVH = 8
KVD = 128
BLK = 16
LANES = 128
ROWS = 80
NEW = 16
EPS = 1e-05
AXES = ("tensor", "side")
F32 = jnp.float32
BF16 = jnp.bfloat16

SMEM = pl.BlockSpec(memory_space=pltpu.SMEM)
VMEM = pl.BlockSpec(memory_space=pltpu.VMEM)
ANY = pl.BlockSpec(memory_space=pl.ANY)
PARAMS = pltpu.CompilerParams(vmem_limit_bytes=48 * 1024 * 1024)


def cost(microseconds):
    return pl.CostEstimate(flops=0, bytes_accessed=microseconds * 3_500_000, transcendentals=0)


def iota(shape, dim):
    return lax.broadcasted_iota(jnp.int32, shape, dim)


def softplus(x):
    return jnp.maximum(x, 0.0) + jnp.log1p(jnp.exp(-jnp.abs(x)))


def silu(x):
    return x / (1.0 + jnp.exp(-x))


def ranks(owners, count, rank_ref):
    def clear(d, carry):
        count[d] = 0
        return carry

    lax.fori_loop(0, count.shape[0], clear, 0)

    def one(r, carry):
        owner = owners[r]
        rank = count[owner]
        rank_ref[r] = rank
        count[owner] = rank + 1
        return carry

    lax.fori_loop(0, owners.shape[0], one, 0)


def pack_kernel(coeff, hidden_in, coeff_new_in, step_in, send, hidden, coeff_new, step_new, sems):
    devices = send.shape[0]
    slots = hidden.shape[0]
    group_devs = devices // GROUPS
    span = coeff.shape[1]
    news = [
        pltpu.make_async_copy(a, b, sems.at[i])
        for i, (a, b) in enumerate(
            ((hidden_in, hidden), (coeff_new_in, coeff_new), (step_in, step_new))
        )
    ]

    def start_of(d):
        return pl.multiple_of((d // group_devs * 2 + lax.rem(d, 2)) * LANES, LANES)

    def piece(d):
        return pltpu.make_async_copy(
            coeff.at[0, :, pl.ds(start_of(d), LANES)],
            send.at[d, pl.ds(0, span), :],
            sems.at[3 + d],
        )

    for copy in news:
        copy.start()

    def begin(d, carry):
        piece(d).start()
        return carry

    lax.fori_loop(0, devices, begin, 0)
    for copy in news:
        copy.wait()

    heads = step_new.shape[2]
    steps = jnp.concatenate([step_new[k] for k in range(slots)], axis=0)
    if heads < LANES:
        steps = jnp.concatenate(
            [steps, jnp.zeros((steps.shape[0], LANES - heads), F32)], axis=1
        )
    steps = jnp.concatenate([steps, jnp.zeros_like(steps)], axis=0)
    padded = steps.shape[1]
    lane = iota((8, LANES), 1)

    def one(d, carry):
        own = pl.multiple_of(d * 2 * LANES, 2 * LANES)
        rows = jnp.concatenate(
            [hidden[k, :, pl.ds(own, 2 * LANES)].astype(F32) for k in range(slots)], axis=0
        )
        tokens = jnp.concatenate(
            [coeff_new[k, :, pl.ds(start_of(d), LANES)].astype(F32) for k in range(slots)], axis=0
        )
        mine = pltpu.roll(steps, lax.rem(padded - d * 4, padded), 1)[:, :LANES]
        high = mine.astype(BF16).astype(F32)
        rest = mine - high
        middle = rest.astype(BF16).astype(F32)
        low = rest - middle
        split = jnp.where(
            lane < 32, high, jnp.where(lane < 64, pltpu.roll(middle, 32, 1), pltpu.roll(low, 64, 1))
        )
        block = jnp.concatenate([rows[:, :LANES], rows[:, LANES:], tokens, split[0:4]], axis=0)
        send[d, span : span + NEW, :] = block.astype(BF16)
        return carry

    lax.fori_loop(0, devices, one, 0, unroll=4)

    def end(d, carry):
        piece(d).wait()
        return carry

    lax.fori_loop(0, devices, end, 0)


def pack_cache_kernel(owners, cache, send, count, source):
    devices = send.shape[0]
    slots = source.shape[0] // devices
    width = cache.shape[2]

    def clear(d, carry):
        count[d] = 0
        for k in range(slots):
            source[d * slots + k] = 0
        return carry

    lax.fori_loop(0, devices, clear, 0)

    def place(r, carry):
        owner = owners[r]
        rank = count[owner]
        source[owner * slots + rank] = r
        count[owner] = rank + 1
        return carry

    lax.fori_loop(0, owners.shape[0], place, 0)

    def one(d, carry):
        kept = jnp.concatenate(
            [cache[source[d * slots + k]].astype(F32) for k in range(slots)], axis=0
        )
        kept = jnp.concatenate(
            [kept[:, c * LANES : (c + 1) * LANES] for c in range(width // LANES)], axis=0
        )
        send[d] = kept.astype(BF16)
        return carry

    lax.fori_loop(0, devices, one, 0, unroll=2)


def spliced(rows, first, second, length):
    columns = rows.shape[1]
    rows = jnp.concatenate([rows, jnp.zeros((ROWS - rows.shape[0], columns), F32)], axis=0)
    place = iota((ROWS, columns), 0)
    return jnp.where(place == length, first, jnp.where(place == length + 1, second, rows))


def conv(rows, taps):
    total = pltpu.roll(rows, 3, 0) * taps[0:1]
    total = total + pltpu.roll(rows, 2, 0) * taps[1:2]
    total = total + pltpu.roll(rows, 1, 0) * taps[2:3]
    total = total + rows * taps[3:4]
    return silu(total).astype(BF16)


def coeff_kernel(owners, lengths, taps_ref, recv, out, count, rank_ref):
    prompts = out.shape[0]
    span = recv.shape[1] - NEW
    devices = recv.shape[0]
    group_devs = devices // GROUPS
    ranks(owners, count, rank_ref)
    me = lax.axis_index(AXES)
    start = pl.multiple_of((me // group_devs * 2 + lax.rem(me, 2)) * LANES, LANES)
    taps = taps_ref[:, pl.ds(start, LANES)].astype(F32)

    def one(r, carry):
        new = recv[owners[r], span : span + NEW, :].astype(F32)
        is_first = rank_ref[r] == 0
        first = jnp.where(is_first, new[8:9], new[10:11])
        second = jnp.where(is_first, new[9:10], new[11:12])
        rows = spliced(recv[r, 0:span, :].astype(F32), first, second, lengths[r])
        out[r] = conv(rows, taps)
        return carry

    lax.fori_loop(0, prompts, one, 0, unroll=2)


def main_kernel(
    owners,
    lengths,
    bias,
    decay,
    skip,
    taps_ref,
    mine,
    other,
    new_ref,
    hidden,
    gate,
    step,
    gated_ref,
    fin,
    count,
    rank_ref,
    tokens,
    dt_ref,
    sum_ref,
):
    prompts, span, columns = hidden.shape
    local_heads = step.shape[0]
    head_size = columns // local_heads
    ranks(owners, count, rank_ref)
    me = lax.axis_index(AXES)
    is_b = lax.rem(me, 2) == 0
    taps = taps_ref[:, pl.ds(pl.multiple_of(me * columns, LANES), columns)].astype(F32)
    fin[...] = jnp.zeros_like(fin)

    def fetch(r, carry):
        new = new_ref[owners[r]].astype(F32)
        is_first = rank_ref[r] == 0
        tokens[0, pl.ds(r, 1), :] = jnp.where(is_first, new[12:13], new[14:15])
        tokens[1, pl.ds(r, 1), :] = jnp.where(is_first, new[13:14], new[15:16])
        return carry

    lax.fori_loop(0, prompts, fetch, 0)

    def widths(r, lens):
        return jnp.where(iota((prompts, LANES), 0) == r, lengths[r], lens)

    lens = lax.fori_loop(0, prompts, widths, jnp.zeros((prompts, LANES), jnp.int32))
    lane = iota((prompts, LANES), 1)
    news = []
    for i in range(2):
        raw = tokens[i]
        news.append(raw + pltpu.roll(raw, LANES - 32, 1) + pltpu.roll(raw, LANES - 64, 1))
    for h in range(local_heads):
        raw = jnp.concatenate([step[h], jnp.zeros((prompts, LANES - span), F32)], axis=1)
        raw = jnp.where(
            lane == lens,
            news[0][:, h : h + 1],
            jnp.where(lane == lens + 1, news[1][:, h : h + 1], raw),
        )
        size = jnp.where(lane < lens + 2, softplus(raw + bias[me * local_heads + h]), 0.0)
        rate = -jnp.exp(jnp.full((1, LANES), decay[me * local_heads + h], F32))
        total = size * rate
        shift = 1
        while shift < LANES:
            total = total + jnp.where(lane >= shift, pltpu.roll(total, shift, 1), 0.0)
            shift *= 2
        dt_ref[:, h, :] = size
        sum_ref[:, h, :] = total

    head_of = iota((1, columns), 1) // head_size
    gain = jnp.zeros((1, columns), F32)
    for h in range(local_heads):
        gain = jnp.where(head_of == h, skip[me * local_heads + h], gain)
    heads_wide = iota((ROWS, columns), 1) // head_size
    place = iota((ROWS, columns), 0)
    lower = iota((ROWS, ROWS), 0) >= iota((ROWS, ROWS), 1)
    column_of = iota((span, LANES), 1)

    def one(r, squares):
        owner = owners[r]
        rank = rank_ref[r]
        length = lengths[r]
        new = new_ref[owner].astype(F32)
        is_first = rank == 0
        token = []
        for i in range(2):
            a = jnp.where(is_first, new[i : i + 1], new[2 + i : 3 + i])
            b = jnp.where(is_first, new[4 + i : 5 + i], new[6 + i : 7 + i])
            token.append(jnp.concatenate([a, b], axis=1))
        u = conv(spliced(hidden[r].astype(F32), token[0], token[1], length), taps)
        here, there = mine[r], other[r]
        b_rows = jnp.where(is_b, here, there)
        c_rows = jnp.where(is_b, there, here)
        scores = lax.dot_general(
            c_rows, b_rows, (((1,), (1,)), ((), ())), preferred_element_type=F32
        )
        sums = sum_ref[r]
        sizes = dt_ref[r]
        turned = sums.T
        out = gain * u.astype(F32)
        for h in range(local_heads):
            gap = turned[:ROWS, h : h + 1] - sums[h : h + 1, :ROWS]
            mix = jnp.where(lower, scores * jnp.exp(gap) * sizes[h : h + 1, :ROWS], 0.0)
            only = jnp.where(heads_wide == h, u, jnp.zeros((), BF16))
            out = out + jnp.dot(mix.astype(BF16), only, preferred_element_type=F32)
        for i in range(2):
            row = jnp.sum(jnp.where(place == length + i, out, 0.0), axis=0, keepdims=True)
            for half in range(2):
                fin[owner, pl.ds(prompts // 2 + 4 * half + 2 * rank + i, 1), :] = row[
                    :, half * LANES : (half + 1) * LANES
                ]
        gated = out[:span] * silu(gate[r].astype(F32))
        gated_ref[r] = gated
        square = jnp.sum(gated * gated, axis=1, keepdims=True)
        return jnp.where(column_of == r, square, squares)

    squares = lax.fori_loop(0, prompts, one, jnp.zeros((span, LANES), F32))
    turned = squares.T
    half = prompts // 2
    packed = jnp.concatenate([turned[0:half, :], turned[half:prompts, :]], axis=1)

    def spread(d, carry):
        fin[d, 0:half, :] = packed
        return carry

    lax.fori_loop(0, fin.shape[0], spread, 0)


def slot_facts(owners, lengths, slots):
    me = lax.axis_index(AXES)

    def one(r, found):
        is_mine = owners[r] == me
        seen = found[-1]
        lens = [
            jnp.where(is_mine & (seen == k), lengths[r], found[k]) for k in range(slots)
        ]
        return (*lens, seen + is_mine.astype(jnp.int32))

    zero = jnp.int32(0)
    return lax.fori_loop(0, owners.shape[0], one, (zero,) * (slots + 1))[:slots]


def cache_kernel(owners, lengths, pages, recv, query, cache_new, pool, attended, rows_ref):
    slots = query.shape[0]
    steps = query.shape[1]
    sources = recv.shape[0]
    width = pool.shape[2]
    parts = width // LANES
    span = sources * (recv.shape[1] // parts) // slots
    offset = 0
    each = recv.shape[1] // parts
    local = each // slots
    lens = slot_facts(owners, lengths, slots)
    keys = sources * each
    row = iota((slots * span, keys), 0)
    key = iota((slots * span, keys), 1)
    slot_of = row // span
    at = lax.rem(row, span)
    wanted = at // local * each + slot_of * local + lax.rem(at, local)
    limit = jnp.where(slot_of == 0, lens[0], lens[1])
    order = jnp.where((key == wanted) & (at < limit), 1.0, 0.0).astype(BF16)
    ask = jnp.concatenate([query[k].astype(F32) for k in range(slots)], axis=0)
    fresh = jnp.concatenate([cache_new[k].astype(F32) for k in range(slots)], axis=0)
    fresh = jnp.concatenate([fresh, jnp.zeros_like(fresh)], axis=0)
    per = query.shape[2] // (KVH * KVD)
    pairs = slots * steps
    count = per * pairs
    ask_slot = lax.rem(iota((count, slots * span), 0), pairs) // steps
    ask_step = lax.rem(iota((count, slots * span), 0), steps)
    key_slot = iota((count, slots * span), 1) // span
    key_at = lax.rem(iota((count, slots * span), 1), span)
    live = (key_slot == ask_slot) & (key_at < jnp.where(ask_slot == 0, lens[0], lens[1]))
    new_row = iota((count, 2 * pairs), 0)
    new_key = iota((count, 2 * pairs), 1)
    new_live = (
        (new_key < pairs)
        & (new_key // steps == lax.rem(new_row, pairs) // steps)
        & (lax.rem(new_key, steps) <= lax.rem(new_row, steps))
    )
    out_slot = lax.rem(iota((count, KVD), 0), pairs) // steps
    filled = jnp.where(out_slot == 0, lens[0], lens[1]) > 0

    for c in range(parts):
        block = recv[:, offset + c * each : offset + (c + 1) * each, :].astype(F32)
        block = block.reshape(keys, LANES).astype(BF16)
        rows_ref[:, c * LANES : (c + 1) * LANES] = jnp.dot(
            order, block, preferred_element_type=F32
        ).astype(BF16)
    blocks = span // BLK
    for k in range(slots):
        for b in range(blocks):
            pool[pages[0, k * blocks + b]] = rows_ref[
                k * span + b * BLK : k * span + (b + 1) * BLK, :
            ]
    contract = (((1,), (1,)), ((), ()))
    answers = []
    for c in range(KVH):
        asked = jnp.concatenate(
            [ask[:, (c * per + g) * KVD : (c * per + g + 1) * KVD] for g in range(per)], axis=0
        ).astype(BF16)
        own = slice(c * KVD, (c + 1) * KVD)
        values = slice((KVH + c) * KVD, (KVH + c + 1) * KVD)
        old = lax.dot_general(asked, rows_ref[:, own], contract, preferred_element_type=F32)
        recent = lax.dot_general(
            asked, fresh[:, own].astype(BF16), contract, preferred_element_type=F32
        )
        old = jnp.where(live, old * KVD ** (-0.5), -jnp.inf)
        recent = jnp.where(new_live, recent * KVD ** (-0.5), -jnp.inf)
        peak = jnp.maximum(
            jnp.max(old, axis=1, keepdims=True), jnp.max(recent, axis=1, keepdims=True)
        )
        old = jnp.exp(old - peak)
        recent = jnp.exp(recent - peak)
        total = jnp.sum(old, axis=1, keepdims=True) + jnp.sum(recent, axis=1, keepdims=True)
        got = jnp.dot(
            (old / total).astype(BF16), rows_ref[:, values], preferred_element_type=F32
        ) + jnp.dot(
            (recent / total).astype(BF16),
            fresh[:, values].astype(BF16),
            preferred_element_type=F32,
        )
        got = jnp.where(filled, got, 0.0)
        answers += [got[g * pairs : (g + 1) * pairs] for g in range(per)]
    whole = jnp.concatenate(answers, axis=1)
    for k in range(slots):
        attended[k] = whole[k * steps : (k + 1) * steps].astype(BF16)


def final_kernel(owners, lengths, gain_ref, fin, gated, new_gate, prefill, mixer):
    prompts, span, columns = gated.shape
    slots = new_gate.shape[0]
    steps = new_gate.shape[1]
    sources = fin.shape[0]
    width = new_gate.shape[2]
    half = prompts // 2
    me = lax.axis_index(AXES)
    total = fin[0, 0:half, :]
    for s in range(1, sources):
        total = total + fin[s, 0:half, :]
    scale = lax.rsqrt(total / width + EPS).T
    gain = gain_ref[:, pl.ds(pl.multiple_of(me * columns, LANES), columns)]
    place = iota((span, columns), 0)
    for r in range(prompts):
        low = 0 if r < half else span
        column = scale[low : low + span, r % half : r % half + 1]
        rows = gated[r] * column * gain
        prefill[r] = jnp.where(place < lengths[r], rows, 0.0).astype(BF16)
    lens = slot_facts(owners, lengths, slots)
    read = jnp.concatenate(
        [
            fin[s, half + pairs : half + pairs + 4, :]
            for s in range(sources)
            for pairs in (0, 4)
        ],
        axis=1,
    )
    gates = jnp.concatenate([new_gate[k].astype(F32) for k in range(slots)], axis=0)
    out = read * silu(gates)
    mean = jnp.mean(out * out, axis=1, keepdims=True)
    out = out * lax.rsqrt(mean + EPS) * gain_ref[...]
    slot_of = iota(out.shape, 0) // steps
    out = jnp.where(jnp.where(slot_of == 0, lens[0], lens[1]) > 0, out, 0.0)
    for k in range(slots):
        mixer[k] = out[k * steps : (k + 1) * steps].astype(BF16)


def local(
    hidden_pre,
    coeff_pre,
    gate_pre,
    step_raw,
    cache_rows,
    lengths,
    owners,
    page_table,
    conv_hidden,
    conv_coeff,
    step_bias,
    decay_log,
    skip_gain,
    norm_gain,
    new_hidden,
    new_coeff,
    new_gate,
    new_step,
    new_query,
    new_cache,
):
    devices = lax.axis_size(AXES)
    prompts, span, columns = hidden_pre.shape
    slots = new_hidden.shape[0]
    local_heads = step_raw.shape[0]
    cache_width = cache_rows.shape[2]
    kept_rows = slots * cache_rows.shape[1] * cache_width // LANES
    per_owner = pltpu.SMEM((devices,), jnp.int32)
    per_prompt = pltpu.SMEM((prompts,), jnp.int32)

    owners = owners[:, 0]
    send = pl.pallas_call(
        pack_kernel,
        out_shape=jax.ShapeDtypeStruct((devices, span + NEW, LANES), BF16),
        in_specs=[ANY, ANY, ANY, ANY],
        out_specs=VMEM,
        scratch_shapes=[
            pltpu.VMEM(new_hidden.shape, BF16),
            pltpu.VMEM(new_coeff.shape, BF16),
            pltpu.VMEM(new_step.shape, F32),
            pltpu.SemaphoreType.DMA((3 + devices,)),
        ],
        name="pack",
    )(coeff_pre, new_hidden, new_coeff, new_step)
    recv = lax.all_to_all(send, AXES, split_axis=0, concat_axis=0, tiled=True)
    kept = pl.pallas_call(
        pack_cache_kernel,
        out_shape=jax.ShapeDtypeStruct((devices, kept_rows, LANES), BF16),
        in_specs=[SMEM, VMEM],
        out_specs=VMEM,
        scratch_shapes=[per_owner, pltpu.SMEM((devices * slots,), jnp.int32)],
        compiler_params=PARAMS,
        cost_estimate=cost(3),
        name="pack_cache",
    )(owners, cache_rows)
    kept, recv = lax.optimization_barrier((kept, recv))
    kept = lax.all_to_all(kept, AXES, split_axis=0, concat_axis=0, tiled=True)

    mine = pl.pallas_call(
        coeff_kernel,
        grid=(1,),
        out_shape=jax.ShapeDtypeStruct((prompts, ROWS, LANES), BF16),
        in_specs=[
            SMEM,
            SMEM,
            VMEM,
            pl.BlockSpec((devices, span + NEW, LANES), lambda i: (0, 0, 0)),
        ],
        out_specs=VMEM,
        scratch_shapes=[per_owner, per_prompt],
        compiler_params=PARAMS,
        cost_estimate=cost(2),
        name="coeff",
    )(owners, lengths, conv_coeff, recv)
    other = lax.ppermute(mine, "side", [(0, 1), (1, 0)])

    new_block = span // NEW
    gated, fin = pl.pallas_call(
        main_kernel,
        grid=(1,),
        out_shape=(
            jax.ShapeDtypeStruct((prompts, span, columns), F32),
            jax.ShapeDtypeStruct((devices, prompts // 2 + 8, LANES), F32),
        ),
        in_specs=[SMEM] * 5
        + [VMEM] * 3
        + [pl.BlockSpec((devices, NEW, LANES), lambda i: (0, new_block, 0))]
        + [VMEM] * 3,
        out_specs=(VMEM, VMEM),
        scratch_shapes=[
            per_owner,
            per_prompt,
            pltpu.VMEM((2, prompts, LANES), F32),
            pltpu.VMEM((prompts, 8, LANES), F32),
            pltpu.VMEM((prompts, 8, LANES), F32),
        ],
        compiler_params=PARAMS,
        cost_estimate=cost(10),
        name="main",
    )(
        owners,
        lengths,
        step_bias,
        decay_log,
        skip_gain,
        conv_hidden,
        mine,
        other,
        recv,
        hidden_pre,
        gate_pre,
        step_raw,
    )
    fin, kept = lax.optimization_barrier((fin, kept))
    fin_got = lax.all_to_all(fin, AXES, split_axis=0, concat_axis=0, tiled=True)

    cache_pool, decode_attention = pl.pallas_call(
        cache_kernel,
        out_shape=(
            jax.ShapeDtypeStruct((page_table.shape[1], BLK, cache_width), BF16),
            jax.ShapeDtypeStruct(new_query.shape, BF16),
        ),
        in_specs=[SMEM, SMEM, SMEM, VMEM, VMEM, VMEM],
        out_specs=(VMEM, VMEM),
        scratch_shapes=[pltpu.VMEM((slots * span, cache_width), BF16)],
        compiler_params=PARAMS,
        cost_estimate=cost(5),
        name="cache",
    )(owners, lengths, page_table, kept, new_query, new_cache)

    prefill_out, decode_mixer = pl.pallas_call(
        final_kernel,
        out_shape=(
            jax.ShapeDtypeStruct(hidden_pre.shape, BF16),
            jax.ShapeDtypeStruct(new_gate.shape, BF16),
        ),
        in_specs=[SMEM, SMEM, VMEM, VMEM, VMEM, VMEM],
        out_specs=(VMEM, VMEM),
        compiler_params=PARAMS,
        name="final",
    )(owners, lengths, norm_gain.reshape(1, -1), fin_got, gated, new_gate)
    return (prefill_out, cache_pool, decode_mixer, decode_attention)


def solution(mesh):
    own = P(("group", "tensor", "side"), None, None)
    placed = (
        P("group", None, ("tensor", "side")),
        own,
        P("group", None, ("tensor", "side")),
        P(("tensor", "side"), "group", None),
        P("group", ("tensor", "side"), None),
        P("group"),
        P("group", None),
        P(("group", "tensor", "side"), None),
        P(),
        P(),
        P(),
        P(),
        P(),
        P(),
        own,
        own,
        own,
        own,
        own,
        own,
    )
    return jax.shard_map(
        local,
        mesh=mesh,
        in_specs=placed,
        out_specs=(P("group", None, ("tensor", "side")), own, own, own),
        check_vma=False,
    )
```

```python
import jax
import jax.numpy as jnp
from jax import lax
from jax.experimental import pallas as pl
from jax.experimental.pallas import tpu as pltpu
from jax.sharding import PartitionSpec as P

GROUPS = 8
CONVK = 4
KVH = 8
KVD = 128
BLK = 16
LANES = 128
ROWS = 80
NEW = 16
EPS = 1e-05
AXES = ("tensor", "side")
F32 = jnp.float32
BF16 = jnp.bfloat16

SMEM = pl.BlockSpec(memory_space=pltpu.SMEM)
VMEM = pl.BlockSpec(memory_space=pltpu.VMEM)
ANY = pl.BlockSpec(memory_space=pl.ANY)
PARAMS = pltpu.CompilerParams(vmem_limit_bytes=48 * 1024 * 1024)


def cost(microseconds):
    return pl.CostEstimate(flops=0, bytes_accessed=microseconds * 3_500_000, transcendentals=0)


def iota(shape, dim):
    return lax.broadcasted_iota(jnp.int32, shape, dim)


def softplus(x):
    return jnp.maximum(x, 0.0) + jnp.log1p(jnp.exp(-jnp.abs(x)))


def silu(x):
    return x / (1.0 + jnp.exp(-x))


def ranks(owners, count, rank_ref):
    def clear(d, carry):
        count[d] = 0
        return carry

    lax.fori_loop(0, count.shape[0], clear, 0)

    def one(r, carry):
        owner = owners[r]
        rank = count[owner]
        rank_ref[r] = rank
        count[owner] = rank + 1
        return carry

    lax.fori_loop(0, owners.shape[0], one, 0)


def pack_kernel(coeff, hidden_in, coeff_new_in, step_in, send, hidden, coeff_new, step_new, sems):
    devices = send.shape[0]
    slots = hidden.shape[0]
    group_devs = devices // GROUPS
    span = coeff.shape[1]
    news = [
        pltpu.make_async_copy(a, b, sems.at[i])
        for i, (a, b) in enumerate(
            ((hidden_in, hidden), (coeff_new_in, coeff_new), (step_in, step_new))
        )
    ]

    def start_of(d):
        return pl.multiple_of((d // group_devs * 2 + lax.rem(d, 2)) * LANES, LANES)

    def piece(d):
        return pltpu.make_async_copy(
            coeff.at[0, :, pl.ds(start_of(d), LANES)],
            send.at[d, pl.ds(0, span), :],
            sems.at[3 + d],
        )

    for copy in news:
        copy.start()

    def begin(d, carry):
        piece(d).start()
        return carry

    lax.fori_loop(0, devices, begin, 0)
    for copy in news:
        copy.wait()

    heads = step_new.shape[2]
    steps = jnp.concatenate([step_new[k] for k in range(slots)], axis=0)
    if heads < LANES:
        steps = jnp.concatenate(
            [steps, jnp.zeros((steps.shape[0], LANES - heads), F32)], axis=1
        )
    steps = jnp.concatenate([steps, jnp.zeros_like(steps)], axis=0)
    padded = steps.shape[1]
    lane = iota((8, LANES), 1)

    def one(d, carry):
        own = pl.multiple_of(d * 2 * LANES, 2 * LANES)
        rows = jnp.concatenate(
            [hidden[k, :, pl.ds(own, 2 * LANES)].astype(F32) for k in range(slots)], axis=0
        )
        tokens = jnp.concatenate(
            [coeff_new[k, :, pl.ds(start_of(d), LANES)].astype(F32) for k in range(slots)], axis=0
        )
        mine = pltpu.roll(steps, lax.rem(padded - d * 4, padded), 1)[:, :LANES]
        high = mine.astype(BF16).astype(F32)
        rest = mine - high
        middle = rest.astype(BF16).astype(F32)
        low = rest - middle
        split = jnp.where(
            lane < 32, high, jnp.where(lane < 64, pltpu.roll(middle, 32, 1), pltpu.roll(low, 64, 1))
        )
        block = jnp.concatenate([rows[:, :LANES], rows[:, LANES:], tokens, split[0:4]], axis=0)
        send[d, span : span + NEW, :] = block.astype(BF16)
        return carry

    lax.fori_loop(0, devices, one, 0, unroll=8)

    def end(d, carry):
        piece(d).wait()
        return carry

    lax.fori_loop(0, devices, end, 0)


def pack_cache_kernel(owners, cache, *refs):
    outs, (count, source) = refs[:-2], refs[-2:]
    devices = count.shape[0]
    slots = source.shape[0] // devices
    width = cache.shape[2]

    def clear(d, carry):
        count[d] = 0
        for k in range(slots):
            source[d * slots + k] = 0
        return carry

    lax.fori_loop(0, devices, clear, 0, unroll=4)

    def place(r, carry):
        owner = owners[r]
        rank = count[owner]
        source[owner * slots + rank] = r
        count[owner] = rank + 1
        return carry

    lax.fori_loop(0, owners.shape[0], place, 0, unroll=4)
    me = lax.axis_index(AXES)
    for m, out in enumerate(outs):
        for x in range(2):
            d = me ^ (2 * m + x)
            kept = jnp.concatenate(
                [cache[source[d * slots + k]].astype(F32) for k in range(slots)], axis=0
            )
            kept = jnp.concatenate(
                [kept[:, c * LANES : (c + 1) * LANES] for c in range(width // LANES)], axis=0
            )
            out[x] = kept.astype(BF16)


def stack_kernel(*refs):
    for m, ref in enumerate(refs[:-1]):
        refs[-1][m] = ref[1]


def spliced(rows, first, second, length):
    columns = rows.shape[1]
    rows = jnp.concatenate([rows, jnp.zeros((ROWS - rows.shape[0], columns), F32)], axis=0)
    place = iota((ROWS, columns), 0)
    return jnp.where(place == length, first, jnp.where(place == length + 1, second, rows))


def conv(rows, taps):
    total = pltpu.roll(rows, 3, 0) * taps[0:1]
    total = total + pltpu.roll(rows, 2, 0) * taps[1:2]
    total = total + pltpu.roll(rows, 1, 0) * taps[2:3]
    total = total + rows * taps[3:4]
    return silu(total).astype(BF16)


def coeff_kernel(owners, lengths, taps_ref, recv, out, count, rank_ref):
    prompts = out.shape[0]
    span = recv.shape[1] - NEW
    devices = recv.shape[0]
    group_devs = devices // GROUPS
    ranks(owners, count, rank_ref)
    me = lax.axis_index(AXES)
    start = pl.multiple_of((me // group_devs * 2 + lax.rem(me, 2)) * LANES, LANES)
    taps = taps_ref[:, pl.ds(start, LANES)].astype(F32)

    def one(r, carry):
        new = recv[owners[r], span : span + NEW, :].astype(F32)
        is_first = rank_ref[r] == 0
        first = jnp.where(is_first, new[8:9], new[10:11])
        second = jnp.where(is_first, new[9:10], new[11:12])
        rows = spliced(recv[r, 0:span, :].astype(F32), first, second, lengths[r])
        out[r] = conv(rows, taps)
        return carry

    lax.fori_loop(0, prompts, one, 0, unroll=4)


def before_kernel(
    lengths, bias, decay, skip, taps_ref, hidden, step, u_ref, tail_ref, head_ref, dt_ref, sum_ref
):
    prompts, span, columns = hidden.shape
    local_heads = step.shape[0]
    me = lax.axis_index(AXES)
    taps = taps_ref[:, pl.ds(pl.multiple_of(me * columns, LANES), columns)].astype(F32)

    def widths(r, lens):
        return jnp.where(iota((prompts, LANES), 0) == r, lengths[r], lens)

    lens = lax.fori_loop(0, prompts, widths, jnp.zeros((prompts, LANES), jnp.int32), unroll=4)
    lane = iota((prompts, LANES), 1)
    for h in range(local_heads):
        raw = jnp.concatenate([step[h], jnp.zeros((prompts, LANES - span), F32)], axis=1)
        size = jnp.where(lane < lens, softplus(raw + bias[me * local_heads + h]), 0.0)
        total = size * -jnp.exp(jnp.full((1, LANES), decay[me * local_heads + h], F32))
        shift = 1
        while shift < span:
            total = total + jnp.where(lane >= shift, pltpu.roll(total, shift, 1), 0.0)
            shift *= 2
        dt_ref[h] = size
        sum_ref[h] = jnp.where(lane < span, total, total[:, span - 1 : span])
    place = iota((span, columns), 0)
    head_of = iota((1, columns), 1) // (columns // local_heads)
    rows = [jnp.zeros((1, columns), F32)] * 3
    for h in range(local_heads):
        given = (skip[me * local_heads + h], bias[me * local_heads + h], decay[me * local_heads + h])
        rows = [jnp.where(head_of == h, x, row) for x, row in zip(given, rows)]
    rows[2] = -jnp.exp(rows[2])
    head_ref[...] = jnp.concatenate([*rows, jnp.zeros((5, columns), F32)], axis=0)

    def one(r, carry):
        raw = hidden[r].astype(F32)
        for j in range(CONVK - 1):
            tail_ref[j, pl.ds(r, 1), :] = jnp.sum(
                jnp.where(place == lengths[r] - 3 + j, raw, 0.0), axis=0, keepdims=True
            )
        longer = jnp.concatenate([raw, jnp.zeros((8, columns), F32)], axis=0)
        u_ref[r] = conv(longer, taps)[0:span]
        return carry

    lax.fori_loop(0, prompts, one, 0, unroll=2)


def main_kernel(
    owners,
    lengths,
    taps_ref,
    mine,
    other,
    new_ref,
    gate,
    u_ref,
    tail_ref,
    consts,
    dt_given,
    sum_given,
    gated_ref,
    fin,
    count,
    rank_ref,
    tokens,
    rows_ref,
    dt_ref,
    sum_ref,
):
    prompts, span, columns = gate.shape
    local_heads = dt_given.shape[0]
    head_size = columns // local_heads
    ranks(owners, count, rank_ref)
    me = lax.axis_index(AXES)
    is_b = lax.rem(me, 2) == 0
    taps = taps_ref[:, pl.ds(pl.multiple_of(me * columns, LANES), columns)].astype(F32)
    fin[...] = jnp.zeros_like(fin)

    def fetch(r, carry):
        new = new_ref[owners[r]].astype(F32)
        is_first = rank_ref[r] == 0
        for i in range(2):
            tokens[i, pl.ds(r, 1), :] = jnp.where(is_first, new[12 + i : 13 + i], new[14 + i : 15 + i])
            low = jnp.where(is_first, new[i : i + 1], new[2 + i : 3 + i])
            high = jnp.where(is_first, new[4 + i : 5 + i], new[6 + i : 7 + i])
            rows_ref[i, pl.ds(r, 1), :] = jnp.concatenate([low, high], axis=1)
        return carry

    lax.fori_loop(0, prompts, fetch, 0, unroll=4)
    raws = [tail_ref[0], tail_ref[1], tail_ref[2], rows_ref[0], rows_ref[1]]
    for i in range(2):
        total = sum(raws[i + k] * taps[k : k + 1] for k in range(CONVK))
        rows_ref[i] = silu(total).astype(BF16).astype(F32)

    def widths(r, lens):
        return jnp.where(iota((prompts, LANES), 0) == r, lengths[r], lens)

    lens = lax.fori_loop(0, prompts, widths, jnp.zeros((prompts, LANES), jnp.int32))
    lane = iota((prompts, LANES), 1)
    news = []
    for i in range(2):
        raw = tokens[i]
        news.append(raw + pltpu.roll(raw, LANES - 32, 1) + pltpu.roll(raw, LANES - 64, 1))
    for h in range(local_heads):
        at = slice(h * head_size, h * head_size + 1)
        rate = consts[2:3, at]
        first, second = [softplus(x[:, h : h + 1] + consts[1:2, at]) for x in news]
        dt_ref[:, h, :] = jnp.where(
            lane == lens, first, jnp.where(lane == lens + 1, second, dt_given[h])
        )
        sum_ref[:, h, :] = (
            sum_given[h]
            + jnp.where(lane >= lens, first * rate, 0.0)
            + jnp.where(lane > lens, second * rate, 0.0)
        )

    gain = consts[0:1, :]
    heads_wide = iota((ROWS, columns), 1) // head_size
    place = iota((ROWS, columns), 0)
    lower = iota((ROWS, ROWS), 0) >= iota((ROWS, ROWS), 1)
    column_of = iota((span, LANES), 1)

    def one(r, squares):
        owner = owners[r]
        rank = rank_ref[r]
        length = lengths[r]
        wide = jnp.concatenate(
            [u_ref[r].astype(F32), jnp.zeros((ROWS - span, columns), F32)], axis=0
        )
        wide = jnp.where(
            place == length,
            rows_ref[0, pl.ds(r, 1), :],
            jnp.where(place == length + 1, rows_ref[1, pl.ds(r, 1), :], wide),
        )
        u = wide.astype(BF16)
        here, there = mine[r], other[r]
        b_rows = jnp.where(is_b, here, there)
        c_rows = jnp.where(is_b, there, here)
        scores = lax.dot_general(
            c_rows, b_rows, (((1,), (1,)), ((), ())), preferred_element_type=F32
        )
        sums = sum_ref[r]
        sizes = dt_ref[r]
        turned = sums.T
        out = gain * wide
        for h in range(local_heads):
            gap = turned[:ROWS, h : h + 1] - sums[h : h + 1, :ROWS]
            mix = jnp.where(lower, scores * jnp.exp(gap) * sizes[h : h + 1, :ROWS], 0.0)
            only = jnp.where(heads_wide == h, u, jnp.zeros((), BF16))
            out = out + jnp.dot(mix.astype(BF16), only, preferred_element_type=F32)
        for i in range(2):
            row = jnp.sum(jnp.where(place == length + i, out, 0.0), axis=0, keepdims=True)
            for half in range(2):
                fin[owner, pl.ds(prompts // 2 + 4 * half + 2 * rank + i, 1), :] = row[
                    :, half * LANES : (half + 1) * LANES
                ]
        gated = out[:span] * silu(gate[r].astype(F32))
        gated_ref[r] = gated
        square = jnp.sum(gated * gated, axis=1, keepdims=True)
        return jnp.where(column_of == r, square, squares)

    squares = lax.fori_loop(0, prompts, one, jnp.zeros((span, LANES), F32), unroll=4)
    turned = squares.T
    half = prompts // 2
    packed = jnp.concatenate([turned[0:half, :], turned[half:prompts, :]], axis=1)

    def spread(d, carry):
        fin[d, 0:half, :] = packed
        return carry

    lax.fori_loop(0, fin.shape[0], spread, 0, unroll=4)


def slot_facts(owners, lengths, slots):
    me = lax.axis_index(AXES)

    def one(r, found):
        is_mine = owners[r] == me
        seen = found[-1]
        lens = [
            jnp.where(is_mine & (seen == k), lengths[r], found[k]) for k in range(slots)
        ]
        return (*lens, seen + is_mine.astype(jnp.int32))

    zero = jnp.int32(0)
    return lax.fori_loop(0, owners.shape[0], one, (zero,) * (slots + 1))[:slots]


def cache_kernel(owners, lengths, pages, query, cache_new, crossed, *refs):
    straight, (pool, attended, rows_ref) = refs[:-3], refs[-3:]
    slots = query.shape[0]
    steps = query.shape[1]
    chips = len(straight)
    sources = 2 * chips
    width = pool.shape[2]
    parts = width // LANES
    span = pool.shape[0] // slots * BLK
    each = crossed.shape[1] // parts
    local = each // slots
    lens = slot_facts(owners, lengths, slots)
    keys = sources * each
    row = iota((slots * span, keys), 0)
    key = iota((slots * span, keys), 1)
    slot_of = row // span
    at = lax.rem(row, span)
    apart = (at // local) ^ lax.axis_index(AXES)
    wanted = (lax.rem(apart, 2) * chips + apart // 2) * each + slot_of * local + lax.rem(at, local)
    limit = jnp.where(slot_of == 0, lens[0], lens[1])
    order = jnp.where((key == wanted) & (at < limit), 1.0, 0.0).astype(BF16)
    ask = jnp.concatenate([query[k].astype(F32) for k in range(slots)], axis=0)
    fresh = jnp.concatenate([cache_new[k].astype(F32) for k in range(slots)], axis=0)
    fresh = jnp.concatenate([fresh, jnp.zeros_like(fresh)], axis=0)
    per = query.shape[2] // (KVH * KVD)
    pairs = slots * steps
    count = per * pairs
    ask_slot = lax.rem(iota((count, slots * span), 0), pairs) // steps
    ask_step = lax.rem(iota((count, slots * span), 0), steps)
    key_slot = iota((count, slots * span), 1) // span
    key_at = lax.rem(iota((count, slots * span), 1), span)
    live = (key_slot == ask_slot) & (key_at < jnp.where(ask_slot == 0, lens[0], lens[1]))
    new_row = iota((count, 2 * pairs), 0)
    new_key = iota((count, 2 * pairs), 1)
    new_live = (
        (new_key < pairs)
        & (new_key // steps == lax.rem(new_row, pairs) // steps)
        & (lax.rem(new_key, steps) <= lax.rem(new_row, steps))
    )
    out_slot = lax.rem(iota((count, KVD), 0), pairs) // steps
    filled = jnp.where(out_slot == 0, lens[0], lens[1]) > 0

    for c in range(parts):
        strip = slice(c * each, (c + 1) * each)
        block = jnp.concatenate(
            [ref[0, strip, :].astype(F32) for ref in straight]
            + [crossed[m, strip, :].astype(F32) for m in range(chips)],
            axis=0,
        ).astype(BF16)
        rows_ref[:, c * LANES : (c + 1) * LANES] = jnp.dot(
            order, block, preferred_element_type=F32
        ).astype(BF16)
    blocks = span // BLK
    for k in range(slots):
        for b in range(blocks):
            pool[pages[0, k * blocks + b]] = rows_ref[
                k * span + b * BLK : k * span + (b + 1) * BLK, :
            ]
    contract = (((1,), (1,)), ((), ()))
    answers = []
    for c in range(KVH):
        asked = jnp.concatenate(
            [ask[:, (c * per + g) * KVD : (c * per + g + 1) * KVD] for g in range(per)], axis=0
        ).astype(BF16)
        own = slice(c * KVD, (c + 1) * KVD)
        values = slice((KVH + c) * KVD, (KVH + c + 1) * KVD)
        old = lax.dot_general(asked, rows_ref[:, own], contract, preferred_element_type=F32)
        recent = lax.dot_general(
            asked, fresh[:, own].astype(BF16), contract, preferred_element_type=F32
        )
        old = jnp.where(live, old * KVD ** (-0.5), -jnp.inf)
        recent = jnp.where(new_live, recent * KVD ** (-0.5), -jnp.inf)
        peak = jnp.maximum(
            jnp.max(old, axis=1, keepdims=True), jnp.max(recent, axis=1, keepdims=True)
        )
        old = jnp.exp(old - peak)
        recent = jnp.exp(recent - peak)
        total = jnp.sum(old, axis=1, keepdims=True) + jnp.sum(recent, axis=1, keepdims=True)
        got = jnp.dot(
            (old / total).astype(BF16), rows_ref[:, values], preferred_element_type=F32
        ) + jnp.dot(
            (recent / total).astype(BF16),
            fresh[:, values].astype(BF16),
            preferred_element_type=F32,
        )
        got = jnp.where(filled, got, 0.0)
        answers += [got[g * pairs : (g + 1) * pairs] for g in range(per)]
    whole = jnp.concatenate(answers, axis=1)
    for k in range(slots):
        attended[k] = whole[k * steps : (k + 1) * steps].astype(BF16)


def final_kernel(owners, lengths, gain_ref, fin, gated, new_gate, prefill, mixer):
    prompts, span, columns = gated.shape
    slots = new_gate.shape[0]
    steps = new_gate.shape[1]
    sources = fin.shape[0]
    width = new_gate.shape[2]
    half = prompts // 2
    me = lax.axis_index(AXES)
    total = fin[0, 0:half, :]
    for s in range(1, sources):
        total = total + fin[s, 0:half, :]
    scale = lax.rsqrt(total / width + EPS).T
    gain = gain_ref[:, pl.ds(pl.multiple_of(me * columns, LANES), columns)]
    place = iota((span, columns), 0)
    for r in range(prompts):
        low = 0 if r < half else span
        column = scale[low : low + span, r % half : r % half + 1]
        rows = gated[r] * column * gain
        prefill[r] = jnp.where(place < lengths[r], rows, 0.0).astype(BF16)
    lens = slot_facts(owners, lengths, slots)
    read = jnp.concatenate(
        [
            fin[s, half + pairs : half + pairs + 4, :]
            for s in range(sources)
            for pairs in (0, 4)
        ],
        axis=1,
    )
    gates = jnp.concatenate([new_gate[k].astype(F32) for k in range(slots)], axis=0)
    out = read * silu(gates)
    mean = jnp.mean(out * out, axis=1, keepdims=True)
    out = out * lax.rsqrt(mean + EPS) * gain_ref[...]
    slot_of = iota(out.shape, 0) // steps
    out = jnp.where(jnp.where(slot_of == 0, lens[0], lens[1]) > 0, out, 0.0)
    for k in range(slots):
        mixer[k] = out[k * steps : (k + 1) * steps].astype(BF16)


def local(
    hidden_pre,
    coeff_pre,
    gate_pre,
    step_raw,
    cache_rows,
    lengths,
    owners,
    page_table,
    conv_hidden,
    conv_coeff,
    step_bias,
    decay_log,
    skip_gain,
    norm_gain,
    new_hidden,
    new_coeff,
    new_gate,
    new_step,
    new_query,
    new_cache,
):
    devices = lax.axis_size(AXES)
    prompts, span, columns = hidden_pre.shape
    slots = new_hidden.shape[0]
    local_heads = step_raw.shape[0]
    cache_width = cache_rows.shape[2]
    kept_rows = slots * cache_rows.shape[1] * cache_width // LANES
    per_owner = pltpu.SMEM((devices,), jnp.int32)
    per_prompt = pltpu.SMEM((prompts,), jnp.int32)

    owners = owners[:, 0]
    send = pl.pallas_call(
        pack_kernel,
        out_shape=jax.ShapeDtypeStruct((devices, span + NEW, LANES), BF16),
        in_specs=[ANY, ANY, ANY, ANY],
        out_specs=VMEM,
        scratch_shapes=[
            pltpu.VMEM(new_hidden.shape, BF16),
            pltpu.VMEM(new_coeff.shape, BF16),
            pltpu.VMEM(new_step.shape, F32),
            pltpu.SemaphoreType.DMA((3 + devices,)),
        ],
        name="pack",
    )(coeff_pre, new_hidden, new_coeff, new_step)
    recv = lax.all_to_all(send, AXES, split_axis=0, concat_axis=0, tiled=True)
    chips = devices // 2
    kept = pl.pallas_call(
        pack_cache_kernel,
        out_shape=(jax.ShapeDtypeStruct((2, kept_rows, LANES), BF16),) * chips,
        in_specs=[SMEM, VMEM],
        out_specs=(VMEM,) * chips,
        scratch_shapes=[per_owner, pltpu.SMEM((devices * slots,), jnp.int32)],
        compiler_params=PARAMS,
        cost_estimate=cost(3),
        name="pack_cache",
    )(owners, cache_rows)
    kept = [kept[0]] + [
        lax.ppermute(kept[m], "tensor", [(i, i ^ m) for i in range(chips)])
        for m in range(1, chips)
    ]
    before = pl.pallas_call(
        before_kernel,
        out_shape=(
            jax.ShapeDtypeStruct((prompts, span, columns), BF16),
            jax.ShapeDtypeStruct((CONVK - 1, prompts, columns), F32),
            jax.ShapeDtypeStruct((8, columns), F32),
            jax.ShapeDtypeStruct((local_heads, prompts, LANES), F32),
            jax.ShapeDtypeStruct((local_heads, prompts, LANES), F32),
        ),
        in_specs=[SMEM] * 4 + [VMEM] * 3,
        out_specs=(VMEM,) * 5,
        compiler_params=PARAMS,
        cost_estimate=cost(4),
        name="before",
    )(lengths, step_bias, decay_log, skip_gain, conv_hidden, hidden_pre, step_raw)
    early = (1, 2)
    recv, sums, *held = lax.optimization_barrier(
        (recv, before[-1], *(kept[m] for m in early))
    )
    before = (*before[:-1], sums)
    for m, block in zip(early, held):
        kept[m] = block

    mine = pl.pallas_call(
        coeff_kernel,
        grid=(1,),
        out_shape=jax.ShapeDtypeStruct((prompts, ROWS, LANES), BF16),
        in_specs=[
            SMEM,
            SMEM,
            VMEM,
            pl.BlockSpec((devices, span + NEW, LANES), lambda i: (0, 0, 0)),
        ],
        out_specs=VMEM,
        scratch_shapes=[per_owner, per_prompt],
        compiler_params=PARAMS,
        cost_estimate=cost(2),
        name="coeff",
    )(owners, lengths, conv_coeff, recv)
    other = lax.ppermute(mine, "side", [(0, 1), (1, 0)])

    new_block = span // NEW
    gated, fin = pl.pallas_call(
        main_kernel,
        grid=(1,),
        out_shape=(
            jax.ShapeDtypeStruct((prompts, span, columns), F32),
            jax.ShapeDtypeStruct((devices, prompts // 2 + 8, LANES), F32),
        ),
        in_specs=[SMEM] * 2
        + [VMEM] * 3
        + [pl.BlockSpec((devices, NEW, LANES), lambda i: (0, new_block, 0))]
        + [VMEM] * 6,
        out_specs=(VMEM, VMEM),
        scratch_shapes=[
            per_owner,
            per_prompt,
            pltpu.VMEM((2, prompts, LANES), F32),
            pltpu.VMEM((2, prompts, columns), F32),
            pltpu.VMEM((prompts, 8, LANES), F32),
            pltpu.VMEM((prompts, 8, LANES), F32),
        ],
        compiler_params=PARAMS,
        cost_estimate=cost(10),
        name="main",
    )(
        owners,
        lengths,
        conv_hidden,
        mine,
        other,
        recv,
        gate_pre,
        *before,
    )
    fin, *kept = lax.optimization_barrier((fin, *kept))
    crossed = pl.pallas_call(
        stack_kernel,
        out_shape=jax.ShapeDtypeStruct((chips, kept_rows, LANES), BF16),
        in_specs=[VMEM] * chips,
        out_specs=VMEM,
        compiler_params=PARAMS,
        cost_estimate=cost(1),
        name="stack",
    )(*kept)
    crossed = lax.ppermute(crossed, "side", [(0, 1), (1, 0)])
    fin_got = lax.all_to_all(fin, AXES, split_axis=0, concat_axis=0, tiled=True)

    cache_pool, decode_attention = pl.pallas_call(
        cache_kernel,
        out_shape=(
            jax.ShapeDtypeStruct((page_table.shape[1], BLK, cache_width), BF16),
            jax.ShapeDtypeStruct(new_query.shape, BF16),
        ),
        in_specs=[SMEM] * 3 + [VMEM] * (3 + chips),
        out_specs=(VMEM, VMEM),
        scratch_shapes=[pltpu.VMEM((slots * span, cache_width), BF16)],
        compiler_params=PARAMS,
        cost_estimate=cost(5),
        name="cache",
    )(owners, lengths, page_table, new_query, new_cache, crossed, *kept)

    fin_got, cache_pool = lax.optimization_barrier((fin_got, cache_pool))
    prefill_out, decode_mixer = pl.pallas_call(
        final_kernel,
        out_shape=(
            jax.ShapeDtypeStruct(hidden_pre.shape, BF16),
            jax.ShapeDtypeStruct(new_gate.shape, BF16),
        ),
        in_specs=[SMEM, SMEM, VMEM, VMEM, VMEM, VMEM],
        out_specs=(VMEM, VMEM),
        compiler_params=PARAMS,
        name="final",
    )(owners, lengths, norm_gain.reshape(1, -1), fin_got, gated, new_gate)
    return (prefill_out, cache_pool, decode_mixer, decode_attention)


def solution(mesh):
    own = P(("group", "tensor", "side"), None, None)
    placed = (
        P("group", None, ("tensor", "side")),
        own,
        P("group", None, ("tensor", "side")),
        P(("tensor", "side"), "group", None),
        P("group", ("tensor", "side"), None),
        P("group"),
        P("group", None),
        P(("group", "tensor", "side"), None),
        P(),
        P(),
        P(),
        P(),
        P(),
        P(),
        own,
        own,
        own,
        own,
        own,
        own,
    )
    return jax.shard_map(
        local,
        mesh=mesh,
        in_specs=placed,
        out_specs=(P("group", None, ("tensor", "side")), own, own, own),
        check_vma=False,
    )
```

```python
import jax
import jax.numpy as jnp
from jax import lax
from jax.experimental import pallas as pl
from jax.experimental.pallas import tpu as pltpu
from jax.sharding import PartitionSpec as P

GROUPS = 8
CONVK = 4
KVH = 8
KVD = 128
BLK = 16
LANES = 128
ROWS = 80
NEW = 16
EPS = 1e-05
AXES = ("tensor", "side")
F32 = jnp.float32
BF16 = jnp.bfloat16

SMEM = pl.BlockSpec(memory_space=pltpu.SMEM)
VMEM = pl.BlockSpec(memory_space=pltpu.VMEM)
ANY = pl.BlockSpec(memory_space=pl.ANY)
PARAMS = pltpu.CompilerParams(vmem_limit_bytes=48 * 1024 * 1024)


def cost(microseconds):
    return pl.CostEstimate(flops=0, bytes_accessed=microseconds * 3_500_000, transcendentals=0)


def iota(shape, dim):
    return lax.broadcasted_iota(jnp.int32, shape, dim)


def div(x, n):
    return x >> (n.bit_length() - 1) if n & (n - 1) == 0 else x // n


def mod(x, n):
    return x & (n - 1) if n & (n - 1) == 0 else lax.rem(x, n)


def softplus(x):
    return jnp.maximum(x, 0.0) + jnp.log1p(jnp.exp(-jnp.abs(x)))


def silu(x):
    return x / (1.0 + jnp.exp(-x))


def ranks(owners, count, rank_ref):
    def clear(d, carry):
        count[d] = 0
        return carry

    lax.fori_loop(0, count.shape[0], clear, 0)

    def one(r, carry):
        owner = owners[r]
        rank = count[owner]
        rank_ref[r] = rank
        count[owner] = rank + 1
        return carry

    lax.fori_loop(0, owners.shape[0], one, 0)


def pack_kernel(coeff, hidden_in, coeff_new_in, step_in, send, hidden, coeff_new, step_new, sems):
    devices = send.shape[0]
    slots = hidden.shape[0]
    group_devs = devices // GROUPS
    span = coeff.shape[1]
    news = [
        pltpu.make_async_copy(a, b, sems.at[i])
        for i, (a, b) in enumerate(
            ((hidden_in, hidden), (coeff_new_in, coeff_new), (step_in, step_new))
        )
    ]

    def start_of(d):
        return pl.multiple_of((d // group_devs * 2 + lax.rem(d, 2)) * LANES, LANES)

    def piece(d):
        return pltpu.make_async_copy(
            coeff.at[0, :, pl.ds(start_of(d), LANES)],
            send.at[d, pl.ds(0, span), :],
            sems.at[3 + d],
        )

    for copy in news:
        copy.start()

    def begin(d, carry):
        piece(d).start()
        return carry

    lax.fori_loop(0, devices, begin, 0)
    for copy in news:
        copy.wait()

    heads = step_new.shape[2]
    steps = jnp.concatenate([step_new[k] for k in range(slots)], axis=0)
    if heads < LANES:
        steps = jnp.concatenate(
            [steps, jnp.zeros((steps.shape[0], LANES - heads), F32)], axis=1
        )
    steps = jnp.concatenate([steps, jnp.zeros_like(steps)], axis=0)
    padded = steps.shape[1]
    lane = iota((8, LANES), 1)

    def one(d, carry):
        own = pl.multiple_of(d * 2 * LANES, 2 * LANES)
        rows = jnp.concatenate(
            [hidden[k, :, pl.ds(own, 2 * LANES)].astype(F32) for k in range(slots)], axis=0
        )
        tokens = jnp.concatenate(
            [coeff_new[k, :, pl.ds(start_of(d), LANES)].astype(F32) for k in range(slots)], axis=0
        )
        mine = pltpu.roll(steps, lax.rem(padded - d * 4, padded), 1)[:, :LANES]
        high = mine.astype(BF16).astype(F32)
        rest = mine - high
        middle = rest.astype(BF16).astype(F32)
        low = rest - middle
        split = jnp.where(
            lane < 32, high, jnp.where(lane < 64, pltpu.roll(middle, 32, 1), pltpu.roll(low, 64, 1))
        )
        block = jnp.concatenate([rows[:, :LANES], rows[:, LANES:], tokens, split[0:4]], axis=0)
        send[d, span : span + NEW, :] = block.astype(BF16)
        return carry

    lax.fori_loop(0, devices, one, 0, unroll=8)

    def end(d, carry):
        piece(d).wait()
        return carry

    lax.fori_loop(0, devices, end, 0)


def pack_cache_kernel(owners, cache, *refs):
    outs, (count, source) = refs[:-2], refs[-2:]
    devices = count.shape[0]
    slots = source.shape[0] // devices
    width = cache.shape[2]

    def clear(d, carry):
        count[d] = 0
        for k in range(slots):
            source[d * slots + k] = 0
        return carry

    lax.fori_loop(0, devices, clear, 0, unroll=4)

    def place(r, carry):
        owner = owners[r]
        rank = count[owner]
        source[owner * slots + rank] = r
        count[owner] = rank + 1
        return carry

    lax.fori_loop(0, owners.shape[0], place, 0, unroll=4)
    me = lax.axis_index(AXES)
    for m, out in enumerate(outs):
        for x in range(2):
            d = me ^ (2 * m + x)
            kept = jnp.concatenate(
                [cache[source[d * slots + k]].astype(F32) for k in range(slots)], axis=0
            )
            kept = jnp.concatenate(
                [kept[:, c * LANES : (c + 1) * LANES] for c in range(width // LANES)], axis=0
            )
            out[x] = kept.astype(BF16)


def stack_kernel(*refs):
    for m, ref in enumerate(refs[:-1]):
        refs[-1][m] = ref[1]


def spliced(rows, first, second, length):
    columns = rows.shape[1]
    rows = jnp.concatenate([rows, jnp.zeros((ROWS - rows.shape[0], columns), F32)], axis=0)
    place = iota((ROWS, columns), 0)
    return jnp.where(place == length, first, jnp.where(place == length + 1, second, rows))


def conv(rows, taps):
    total = pltpu.roll(rows, 3, 0) * taps[0:1]
    total = total + pltpu.roll(rows, 2, 0) * taps[1:2]
    total = total + pltpu.roll(rows, 1, 0) * taps[2:3]
    total = total + rows * taps[3:4]
    return silu(total).astype(BF16)


def coeff_kernel(owners, lengths, taps_ref, recv, out, count, rank_ref):
    prompts = out.shape[0]
    span = recv.shape[1] - NEW
    devices = recv.shape[0]
    group_devs = devices // GROUPS
    ranks(owners, count, rank_ref)
    me = lax.axis_index(AXES)
    start = pl.multiple_of((me // group_devs * 2 + lax.rem(me, 2)) * LANES, LANES)
    taps = taps_ref[:, pl.ds(start, LANES)].astype(F32)

    def one(r, carry):
        new = recv[owners[r], span : span + NEW, :].astype(F32)
        is_first = rank_ref[r] == 0
        first = jnp.where(is_first, new[8:9], new[10:11])
        second = jnp.where(is_first, new[9:10], new[11:12])
        rows = spliced(recv[r, 0:span, :].astype(F32), first, second, lengths[r])
        out[r] = conv(rows, taps)
        return carry

    lax.fori_loop(0, prompts, one, 0, unroll=4)


def before_kernel(
    lengths, bias, decay, skip, taps_ref, hidden, step, u_ref, tail_ref, head_ref, dt_ref, sum_ref
):
    prompts, span, columns = hidden.shape
    local_heads = step.shape[0]
    me = lax.axis_index(AXES)
    taps = taps_ref[:, pl.ds(pl.multiple_of(me * columns, LANES), columns)].astype(F32)

    def widths(r, lens):
        return jnp.where(iota((prompts, LANES), 0) == r, lengths[r], lens)

    lens = lax.fori_loop(0, prompts, widths, jnp.zeros((prompts, LANES), jnp.int32), unroll=4)
    lane = iota((prompts, LANES), 1)
    for h in range(local_heads):
        raw = jnp.concatenate([step[h], jnp.zeros((prompts, LANES - span), F32)], axis=1)
        size = jnp.where(lane < lens, softplus(raw + bias[me * local_heads + h]), 0.0)
        total = size * -jnp.exp(jnp.full((1, LANES), decay[me * local_heads + h], F32))
        shift = 1
        while shift < span:
            total = total + jnp.where(lane >= shift, pltpu.roll(total, shift, 1), 0.0)
            shift *= 2
        dt_ref[h] = size
        sum_ref[h] = jnp.where(lane < span, total, total[:, span - 1 : span])
    place = iota((span, columns), 0)
    head_of = iota((1, columns), 1) // (columns // local_heads)
    rows = [jnp.zeros((1, columns), F32)] * 3
    for h in range(local_heads):
        given = (skip[me * local_heads + h], bias[me * local_heads + h], decay[me * local_heads + h])
        rows = [jnp.where(head_of == h, x, row) for x, row in zip(given, rows)]
    rows[2] = -jnp.exp(rows[2])
    head_ref[...] = jnp.concatenate([*rows, jnp.zeros((5, columns), F32)], axis=0)

    def one(r, carry):
        raw = hidden[r].astype(F32)
        for j in range(CONVK - 1):
            tail_ref[j, pl.ds(r, 1), :] = jnp.sum(
                jnp.where(place == lengths[r] - 3 + j, raw, 0.0), axis=0, keepdims=True
            )
        longer = jnp.concatenate([raw, jnp.zeros((8, columns), F32)], axis=0)
        u_ref[r] = conv(longer, taps)[0:span]
        return carry

    lax.fori_loop(0, prompts, one, 0, unroll=2)


def main_kernel(
    owners,
    lengths,
    taps_ref,
    mine,
    other,
    new_ref,
    gate,
    u_ref,
    tail_ref,
    consts,
    dt_given,
    sum_given,
    gated_ref,
    fin_out,
    fin,
    count,
    rank_ref,
    tokens,
    rows_ref,
    dt_ref,
    sum_ref,
):
    prompts, span, columns = gate.shape
    local_heads = dt_given.shape[0]
    head_size = columns // local_heads
    ranks(owners, count, rank_ref)
    me = lax.axis_index(AXES)
    is_b = lax.rem(me, 2) == 0
    taps = taps_ref[:, pl.ds(pl.multiple_of(me * columns, LANES), columns)].astype(F32)
    fin[...] = jnp.zeros_like(fin)

    def fetch(r, carry):
        new = new_ref[owners[r]].astype(F32)
        is_first = rank_ref[r] == 0
        for i in range(2):
            tokens[i, pl.ds(r, 1), :] = jnp.where(is_first, new[12 + i : 13 + i], new[14 + i : 15 + i])
            low = jnp.where(is_first, new[i : i + 1], new[2 + i : 3 + i])
            high = jnp.where(is_first, new[4 + i : 5 + i], new[6 + i : 7 + i])
            rows_ref[i, pl.ds(r, 1), :] = jnp.concatenate([low, high], axis=1)
        return carry

    lax.fori_loop(0, prompts, fetch, 0, unroll=4)
    raws = [tail_ref[0], tail_ref[1], tail_ref[2], rows_ref[0], rows_ref[1]]
    for i in range(2):
        total = sum(raws[i + k] * taps[k : k + 1] for k in range(CONVK))
        rows_ref[i] = silu(total).astype(BF16).astype(F32)

    def widths(r, lens):
        return jnp.where(iota((prompts, LANES), 0) == r, lengths[r], lens)

    lens = lax.fori_loop(0, prompts, widths, jnp.zeros((prompts, LANES), jnp.int32))
    lane = iota((prompts, LANES), 1)
    news = []
    for i in range(2):
        raw = tokens[i]
        news.append(raw + pltpu.roll(raw, LANES - 32, 1) + pltpu.roll(raw, LANES - 64, 1))
    for h in range(local_heads):
        at = slice(h * head_size, h * head_size + 1)
        rate = consts[2:3, at]
        first, second = [softplus(x[:, h : h + 1] + consts[1:2, at]) for x in news]
        dt_ref[:, h, :] = jnp.where(
            lane == lens, first, jnp.where(lane == lens + 1, second, dt_given[h])
        )
        sum_ref[:, h, :] = (
            sum_given[h]
            + jnp.where(lane >= lens, first * rate, 0.0)
            + jnp.where(lane > lens, second * rate, 0.0)
        )

    gain = consts[0:1, :]
    heads_wide = div(iota((ROWS, columns), 1), head_size)
    place = iota((ROWS, columns), 0)
    lower = iota((ROWS, ROWS), 0) >= iota((ROWS, ROWS), 1)
    column_of = iota((span, LANES), 1)

    def one(r, squares):
        owner = owners[r]
        rank = rank_ref[r]
        length = lengths[r]
        wide = jnp.concatenate(
            [u_ref[r].astype(F32), jnp.zeros((ROWS - span, columns), F32)], axis=0
        )
        wide = jnp.where(
            place == length,
            rows_ref[0, pl.ds(r, 1), :],
            jnp.where(place == length + 1, rows_ref[1, pl.ds(r, 1), :], wide),
        )
        u = wide.astype(BF16)
        here, there = mine[r], other[r]
        b_rows = jnp.where(is_b, here, there)
        c_rows = jnp.where(is_b, there, here)
        scores = lax.dot_general(
            c_rows, b_rows, (((1,), (1,)), ((), ())), preferred_element_type=F32
        )
        sums = sum_ref[r]
        sizes = dt_ref[r]
        turned = sums.T
        out = gain * wide
        for h in range(local_heads):
            gap = turned[:ROWS, h : h + 1] - sums[h : h + 1, :ROWS]
            mix = jnp.where(lower, scores * jnp.exp(gap) * sizes[h : h + 1, :ROWS], 0.0)
            only = jnp.where(heads_wide == h, u, jnp.zeros((), BF16))
            out = out + jnp.dot(mix.astype(BF16), only, preferred_element_type=F32)
        for i in range(2):
            row = jnp.sum(jnp.where(place == length + i, out, 0.0), axis=0, keepdims=True)
            for half in range(2):
                fin[owner, pl.ds(4 * half + 2 * rank + i, 1), :] = row[
                    :, half * LANES : (half + 1) * LANES
                ]
        gated = out[:span] * silu(gate[r].astype(F32))
        gated_ref[r] = gated
        square = jnp.sum(gated * gated, axis=1, keepdims=True)
        return jnp.where(column_of == r, square, squares)

    squares = lax.fori_loop(0, prompts, one, jnp.zeros((span, LANES), F32), unroll=4)
    turned = squares.T
    half = prompts // 2
    packed = jnp.concatenate([turned[0:half, :], turned[half:prompts, :]], axis=1)

    high = packed.astype(BF16).astype(F32)
    split = (high, packed - high)

    def spread(d, carry):
        fin_out[d] = jnp.concatenate([*split, fin[d]], axis=0).astype(BF16)
        return carry

    lax.fori_loop(0, fin.shape[0], spread, 0, unroll=4)


def slot_facts(owners, lengths, slots):
    me = lax.axis_index(AXES)

    def one(r, found):
        is_mine = owners[r] == me
        seen = found[-1]
        lens = [
            jnp.where(is_mine & (seen == k), lengths[r], found[k]) for k in range(slots)
        ]
        return (*lens, seen + is_mine.astype(jnp.int32))

    zero = jnp.int32(0)
    return lax.fori_loop(0, owners.shape[0], one, (zero,) * (slots + 1), unroll=8)[:slots]


def cache_kernel(owners, lengths, pages, query, cache_new, crossed, *refs):
    straight, (pool, attended, rows_ref) = refs[:-3], refs[-3:]
    slots = query.shape[0]
    steps = query.shape[1]
    chips = len(straight)
    sources = 2 * chips
    width = pool.shape[2]
    parts = width // LANES
    span = pool.shape[0] // slots * BLK
    each = crossed.shape[1] // parts
    local = each // slots
    lens = slot_facts(owners, lengths, slots)
    keys = sources * each
    key = iota((1, keys), 1)
    block_of = div(key, each)
    apart = mod(block_of, chips) * 2 + div(block_of, chips)
    slot_of = div(mod(key, each), local)
    at = (apart ^ lax.axis_index(AXES)) * local + mod(key, local)
    wanted = jnp.where(at < jnp.where(slot_of == 0, lens[0], lens[1]), slot_of * span + at, -1)
    order = jnp.where(iota((slots * span, keys), 0) == wanted, 1.0, 0.0).astype(BF16)
    ask = jnp.concatenate([query[k].astype(F32) for k in range(slots)], axis=0)
    fresh = jnp.concatenate([cache_new[k].astype(F32) for k in range(slots)], axis=0)
    fresh = jnp.concatenate([fresh, jnp.zeros_like(fresh)], axis=0)
    per = query.shape[2] // (KVH * KVD)
    pairs = slots * steps
    count = per * pairs
    row = iota((count, 1), 0)
    ask_slot, ask_step = div(mod(row, pairs), steps), mod(row, steps)
    key = iota((1, slots * span), 1)
    is_live = mod(key, span) < jnp.where(div(key, span) == 0, lens[0], lens[1])
    live = ask_slot == jnp.where(is_live, div(key, span), -1)
    key = iota((1, 2 * pairs), 1)
    new_live = (ask_slot == jnp.where(key < pairs, div(key, steps), -1)) & (
        mod(key, steps) <= ask_step
    )
    filled = jnp.where(ask_slot == 0, lens[0], lens[1]) > 0

    for c in range(parts):
        strip = slice(c * each, (c + 1) * each)
        block = jnp.concatenate(
            [ref[0, strip, :].astype(F32) for ref in straight]
            + [crossed[m, strip, :].astype(F32) for m in range(chips)],
            axis=0,
        ).astype(BF16)
        rows_ref[:, c * LANES : (c + 1) * LANES] = jnp.dot(
            order, block, preferred_element_type=F32
        ).astype(BF16)
    blocks = span // BLK
    for k in range(slots):
        for b in range(blocks):
            pool[pages[0, k * blocks + b]] = rows_ref[
                k * span + b * BLK : k * span + (b + 1) * BLK, :
            ]
    contract = (((1,), (1,)), ((), ()))
    answers = []
    for c in range(KVH):
        asked = jnp.concatenate(
            [ask[:, (c * per + g) * KVD : (c * per + g + 1) * KVD] for g in range(per)], axis=0
        ).astype(BF16)
        own = slice(c * KVD, (c + 1) * KVD)
        values = slice((KVH + c) * KVD, (KVH + c + 1) * KVD)
        old = lax.dot_general(asked, rows_ref[:, own], contract, preferred_element_type=F32)
        recent = lax.dot_general(
            asked, fresh[:, own].astype(BF16), contract, preferred_element_type=F32
        )
        old = jnp.where(live, old * KVD ** (-0.5), -jnp.inf)
        recent = jnp.where(new_live, recent * KVD ** (-0.5), -jnp.inf)
        peak = jnp.maximum(
            jnp.max(old, axis=1, keepdims=True), jnp.max(recent, axis=1, keepdims=True)
        )
        old = jnp.exp(old - peak)
        recent = jnp.exp(recent - peak)
        total = jnp.sum(old, axis=1, keepdims=True) + jnp.sum(recent, axis=1, keepdims=True)
        got = jnp.dot(
            (old / total).astype(BF16), rows_ref[:, values], preferred_element_type=F32
        ) + jnp.dot(
            (recent / total).astype(BF16),
            fresh[:, values].astype(BF16),
            preferred_element_type=F32,
        )
        got = jnp.where(filled, got, 0.0)
        answers += [got[g * pairs : (g + 1) * pairs] for g in range(per)]
    whole = jnp.concatenate(answers, axis=1)
    for k in range(slots):
        attended[k] = whole[k * steps : (k + 1) * steps].astype(BF16)


def final_kernel(owners, lengths, gain_ref, fin, gated, new_gate, prefill, mixer):
    prompts, span, columns = gated.shape
    slots = new_gate.shape[0]
    steps = new_gate.shape[1]
    sources = fin.shape[0]
    width = new_gate.shape[2]
    half = prompts // 2
    me = lax.axis_index(AXES)
    blocks = [fin[s].astype(F32) for s in range(sources)]
    total = sum(x[half : 2 * half] for x in blocks) + sum(x[0:half] for x in blocks)
    scale = lax.rsqrt(total / width + EPS).T
    gain = gain_ref[:, pl.ds(pl.multiple_of(me * columns, LANES), columns)]
    place = iota((span, columns), 0)
    for r in range(prompts):
        low = 0 if r < half else span
        column = scale[low : low + span, r % half : r % half + 1]
        rows = gated[r] * column * gain
        prefill[r] = jnp.where(place < lengths[r], rows, 0.0).astype(BF16)
    lens = slot_facts(owners, lengths, slots)
    read = jnp.concatenate(
        [
            block[2 * half + pairs : 2 * half + pairs + 4]
            for block in blocks
            for pairs in (0, 4)
        ],
        axis=1,
    )
    gates = jnp.concatenate([new_gate[k].astype(F32) for k in range(slots)], axis=0)
    out = read * silu(gates)
    mean = jnp.mean(out * out, axis=1, keepdims=True)
    out = out * lax.rsqrt(mean + EPS) * gain_ref[...]
    slot_of = div(iota((out.shape[0], 1), 0), steps)
    out = jnp.where(jnp.where(slot_of == 0, lens[0], lens[1]) > 0, out, 0.0)
    for k in range(slots):
        mixer[k] = out[k * steps : (k + 1) * steps].astype(BF16)


def local(
    hidden_pre,
    coeff_pre,
    gate_pre,
    step_raw,
    cache_rows,
    lengths,
    owners,
    page_table,
    conv_hidden,
    conv_coeff,
    step_bias,
    decay_log,
    skip_gain,
    norm_gain,
    new_hidden,
    new_coeff,
    new_gate,
    new_step,
    new_query,
    new_cache,
):
    devices = lax.axis_size(AXES)
    prompts, span, columns = hidden_pre.shape
    slots = new_hidden.shape[0]
    local_heads = step_raw.shape[0]
    cache_width = cache_rows.shape[2]
    kept_rows = slots * cache_rows.shape[1] * cache_width // LANES
    per_owner = pltpu.SMEM((devices,), jnp.int32)
    per_prompt = pltpu.SMEM((prompts,), jnp.int32)

    owners = owners[:, 0]
    send = pl.pallas_call(
        pack_kernel,
        out_shape=jax.ShapeDtypeStruct((devices, span + NEW, LANES), BF16),
        in_specs=[ANY, ANY, ANY, ANY],
        out_specs=VMEM,
        scratch_shapes=[
            pltpu.VMEM(new_hidden.shape, BF16),
            pltpu.VMEM(new_coeff.shape, BF16),
            pltpu.VMEM(new_step.shape, F32),
            pltpu.SemaphoreType.DMA((3 + devices,)),
        ],
        name="pack",
    )(coeff_pre, new_hidden, new_coeff, new_step)
    recv = lax.all_to_all(send, AXES, split_axis=0, concat_axis=0, tiled=True)
    chips = devices // 2
    kept = pl.pallas_call(
        pack_cache_kernel,
        out_shape=(jax.ShapeDtypeStruct((2, kept_rows, LANES), BF16),) * chips,
        in_specs=[SMEM, VMEM],
        out_specs=(VMEM,) * chips,
        scratch_shapes=[per_owner, pltpu.SMEM((devices * slots,), jnp.int32)],
        compiler_params=PARAMS,
        cost_estimate=cost(3),
        name="pack_cache",
    )(owners, cache_rows)
    kept = [kept[0]] + [
        lax.ppermute(kept[m], "tensor", [(i, i ^ m) for i in range(chips)])
        for m in range(1, chips)
    ]
    before = pl.pallas_call(
        before_kernel,
        out_shape=(
            jax.ShapeDtypeStruct((prompts, span, columns), BF16),
            jax.ShapeDtypeStruct((CONVK - 1, prompts, columns), F32),
            jax.ShapeDtypeStruct((8, columns), F32),
            jax.ShapeDtypeStruct((local_heads, prompts, LANES), F32),
            jax.ShapeDtypeStruct((local_heads, prompts, LANES), F32),
        ),
        in_specs=[SMEM] * 4 + [VMEM] * 3,
        out_specs=(VMEM,) * 5,
        compiler_params=PARAMS,
        cost_estimate=cost(4),
        name="before",
    )(lengths, step_bias, decay_log, skip_gain, conv_hidden, hidden_pre, step_raw)
    early = (1, 2)
    recv, sums, *held = lax.optimization_barrier(
        (recv, before[-1], *(kept[m] for m in early))
    )
    before = (*before[:-1], sums)
    for m, block in zip(early, held):
        kept[m] = block

    mine = pl.pallas_call(
        coeff_kernel,
        grid=(1,),
        out_shape=jax.ShapeDtypeStruct((prompts, ROWS, LANES), BF16),
        in_specs=[
            SMEM,
            SMEM,
            VMEM,
            pl.BlockSpec((devices, span + NEW, LANES), lambda i: (0, 0, 0)),
        ],
        out_specs=VMEM,
        scratch_shapes=[per_owner, per_prompt],
        compiler_params=PARAMS,
        cost_estimate=cost(2),
        name="coeff",
    )(owners, lengths, conv_coeff, recv)
    other = lax.ppermute(mine, "side", [(0, 1), (1, 0)])

    new_block = span // NEW
    gated, fin = pl.pallas_call(
        main_kernel,
        grid=(1,),
        out_shape=(
            jax.ShapeDtypeStruct((prompts, span, columns), F32),
            jax.ShapeDtypeStruct((devices, prompts + 8, LANES), BF16),
        ),
        in_specs=[SMEM] * 2
        + [VMEM] * 3
        + [pl.BlockSpec((devices, NEW, LANES), lambda i: (0, new_block, 0))]
        + [VMEM] * 6,
        out_specs=(VMEM, VMEM),
        scratch_shapes=[
            pltpu.VMEM((devices, 8, LANES), F32),
            per_owner,
            per_prompt,
            pltpu.VMEM((2, prompts, LANES), F32),
            pltpu.VMEM((2, prompts, columns), F32),
            pltpu.VMEM((prompts, 8, LANES), F32),
            pltpu.VMEM((prompts, 8, LANES), F32),
        ],
        compiler_params=PARAMS,
        cost_estimate=cost(10),
        name="main",
    )(
        owners,
        lengths,
        conv_hidden,
        mine,
        other,
        recv,
        gate_pre,
        *before,
    )
    fin, *kept = lax.optimization_barrier((fin, *kept))
    crossed = pl.pallas_call(
        stack_kernel,
        out_shape=jax.ShapeDtypeStruct((chips, kept_rows, LANES), BF16),
        in_specs=[VMEM] * chips,
        out_specs=VMEM,
        compiler_params=PARAMS,
        cost_estimate=cost(1),
        name="stack",
    )(*kept)
    crossed = lax.ppermute(crossed, "side", [(0, 1), (1, 0)])
    fin_got = lax.all_to_all(fin, AXES, split_axis=0, concat_axis=0, tiled=True)

    cache_pool, decode_attention = pl.pallas_call(
        cache_kernel,
        out_shape=(
            jax.ShapeDtypeStruct((page_table.shape[1], BLK, cache_width), BF16),
            jax.ShapeDtypeStruct(new_query.shape, BF16),
        ),
        in_specs=[SMEM] * 3 + [VMEM] * (3 + chips),
        out_specs=(VMEM, VMEM),
        scratch_shapes=[pltpu.VMEM((slots * span, cache_width), BF16)],
        compiler_params=PARAMS,
        cost_estimate=cost(5),
        name="cache",
    )(owners, lengths, page_table, new_query, new_cache, crossed, *kept)

    fin_got, cache_pool = lax.optimization_barrier((fin_got, cache_pool))
    prefill_out, decode_mixer = pl.pallas_call(
        final_kernel,
        out_shape=(
            jax.ShapeDtypeStruct(hidden_pre.shape, BF16),
            jax.ShapeDtypeStruct(new_gate.shape, BF16),
        ),
        in_specs=[SMEM, SMEM, VMEM, VMEM, VMEM, VMEM],
        out_specs=(VMEM, VMEM),
        compiler_params=PARAMS,
        name="final",
    )(owners, lengths, norm_gain.reshape(1, -1), fin_got, gated, new_gate)
    return (prefill_out, cache_pool, decode_mixer, decode_attention)


def solution(mesh):
    own = P(("group", "tensor", "side"), None, None)
    placed = (
        P("group", None, ("tensor", "side")),
        own,
        P("group", None, ("tensor", "side")),
        P(("tensor", "side"), "group", None),
        P("group", ("tensor", "side"), None),
        P("group"),
        P("group", None),
        P(("group", "tensor", "side"), None),
        P(),
        P(),
        P(),
        P(),
        P(),
        P(),
        own,
        own,
        own,
        own,
        own,
        own,
    )
    return jax.shard_map(
        local,
        mesh=mesh,
        in_specs=placed,
        out_specs=(P("group", None, ("tensor", "side")), own, own, own),
        check_vma=False,
    )
```

```python
import jax
import jax.numpy as jnp
from jax import lax
from jax.experimental import pallas as pl
from jax.experimental.pallas import tpu as pltpu
from jax.sharding import PartitionSpec as P

GROUPS = 8
CONVK = 4
KVH = 8
KVD = 128
BLK = 16
LANES = 128
ROWS = 80
NEW = 16
EPS = 1e-05
AXES = ("tensor", "side")
F32 = jnp.float32
BF16 = jnp.bfloat16

SMEM = pl.BlockSpec(memory_space=pltpu.SMEM)
VMEM = pl.BlockSpec(memory_space=pltpu.VMEM)
ANY = pl.BlockSpec(memory_space=pl.ANY)
PARAMS = pltpu.CompilerParams(vmem_limit_bytes=48 * 1024 * 1024)


def cost(microseconds):
    return pl.CostEstimate(flops=0, bytes_accessed=microseconds * 3_500_000, transcendentals=0)


def iota(shape, dim):
    return lax.broadcasted_iota(jnp.int32, shape, dim)


def div(x, n):
    return x >> (n.bit_length() - 1) if n & (n - 1) == 0 else x // n


def mod(x, n):
    return x & (n - 1) if n & (n - 1) == 0 else lax.rem(x, n)


def softplus(x):
    return jnp.maximum(x, 0.0) + jnp.log1p(jnp.exp(-jnp.abs(x)))


def silu(x):
    return x / (1.0 + jnp.exp(-x))


def ranks(owners, count, rank_ref):
    def clear(d, carry):
        count[d] = 0
        return carry

    lax.fori_loop(0, count.shape[0], clear, 0)

    def one(r, carry):
        owner = owners[r]
        rank = count[owner]
        rank_ref[r] = rank
        count[owner] = rank + 1
        return carry

    lax.fori_loop(0, owners.shape[0], one, 0)


def pack_kernel(coeff, hidden_in, coeff_new_in, step_in, send, hidden, coeff_new, step_new, sems):
    devices = send.shape[0]
    slots = hidden.shape[0]
    group_devs = devices // GROUPS
    span = coeff.shape[1]
    news = [
        pltpu.make_async_copy(a, b, sems.at[i])
        for i, (a, b) in enumerate(
            ((hidden_in, hidden), (coeff_new_in, coeff_new), (step_in, step_new))
        )
    ]

    def start_of(d):
        return pl.multiple_of((d // group_devs * 2 + lax.rem(d, 2)) * LANES, LANES)

    def piece(d):
        return pltpu.make_async_copy(
            coeff.at[0, :, pl.ds(start_of(d), LANES)],
            send.at[d, pl.ds(0, span), :],
            sems.at[3 + d],
        )

    for copy in news:
        copy.start()

    def begin(d, carry):
        piece(d).start()
        return carry

    lax.fori_loop(0, devices, begin, 0)
    for copy in news:
        copy.wait()

    heads = step_new.shape[2]
    steps = jnp.concatenate([step_new[k] for k in range(slots)], axis=0)
    if heads < LANES:
        steps = jnp.concatenate(
            [steps, jnp.zeros((steps.shape[0], LANES - heads), F32)], axis=1
        )
    steps = jnp.concatenate([steps, jnp.zeros_like(steps)], axis=0)
    padded = steps.shape[1]
    lane = iota((8, LANES), 1)

    def one(d, carry):
        own = pl.multiple_of(d * 2 * LANES, 2 * LANES)
        rows = jnp.concatenate(
            [hidden[k, :, pl.ds(own, 2 * LANES)].astype(F32) for k in range(slots)], axis=0
        )
        tokens = jnp.concatenate(
            [coeff_new[k, :, pl.ds(start_of(d), LANES)].astype(F32) for k in range(slots)], axis=0
        )
        mine = pltpu.roll(steps, lax.rem(padded - d * 4, padded), 1)[:, :LANES]
        high = mine.astype(BF16).astype(F32)
        rest = mine - high
        middle = rest.astype(BF16).astype(F32)
        low = rest - middle
        split = jnp.where(
            lane < 32, high, jnp.where(lane < 64, pltpu.roll(middle, 32, 1), pltpu.roll(low, 64, 1))
        )
        block = jnp.concatenate([rows[:, :LANES], rows[:, LANES:], tokens, split[0:4]], axis=0)
        send[d, span : span + NEW, :] = block.astype(BF16)
        return carry

    lax.fori_loop(0, devices, one, 0, unroll=8)

    def end(d, carry):
        piece(d).wait()
        return carry

    lax.fori_loop(0, devices, end, 0)


def pack_cache_kernel(owners, cache, *refs):
    outs, (count, source) = refs[:-2], refs[-2:]
    devices = count.shape[0]
    slots = source.shape[0] // devices
    width = cache.shape[2]

    def clear(d, carry):
        count[d] = 0
        for k in range(slots):
            source[d * slots + k] = 0
        return carry

    lax.fori_loop(0, devices, clear, 0, unroll=4)

    def place(r, carry):
        owner = owners[r]
        rank = count[owner]
        source[owner * slots + rank] = r
        count[owner] = rank + 1
        return carry

    lax.fori_loop(0, owners.shape[0], place, 0, unroll=4)
    me = lax.axis_index(AXES)
    for m, out in enumerate(outs):
        for x in range(2):
            d = me ^ (2 * m + x)
            kept = jnp.concatenate(
                [cache[source[d * slots + k]].astype(F32) for k in range(slots)], axis=0
            )
            kept = jnp.concatenate(
                [kept[:, c * LANES : (c + 1) * LANES] for c in range(width // LANES)], axis=0
            )
            out[x] = kept.astype(BF16)


def stack_kernel(*refs):
    for m, ref in enumerate(refs[:-1]):
        refs[-1][m] = ref[1]


def spliced(rows, first, second, length):
    columns = rows.shape[1]
    rows = jnp.concatenate([rows, jnp.zeros((ROWS - rows.shape[0], columns), F32)], axis=0)
    place = iota((ROWS, columns), 0)
    return jnp.where(place == length, first, jnp.where(place == length + 1, second, rows))


def conv(rows, taps):
    total = pltpu.roll(rows, 3, 0) * taps[0:1]
    total = total + pltpu.roll(rows, 2, 0) * taps[1:2]
    total = total + pltpu.roll(rows, 1, 0) * taps[2:3]
    total = total + rows * taps[3:4]
    return silu(total).astype(BF16)


def coeff_kernel(owners, lengths, taps_ref, recv, out, count, rank_ref):
    prompts = out.shape[0]
    span = recv.shape[1] - NEW
    devices = recv.shape[0]
    group_devs = devices // GROUPS
    ranks(owners, count, rank_ref)
    me = lax.axis_index(AXES)
    start = pl.multiple_of((me // group_devs * 2 + lax.rem(me, 2)) * LANES, LANES)
    taps = taps_ref[:, pl.ds(start, LANES)].astype(F32)

    def one(r, carry):
        new = recv[owners[r], span : span + NEW, :].astype(F32)
        is_first = rank_ref[r] == 0
        first = jnp.where(is_first, new[8:9], new[10:11])
        second = jnp.where(is_first, new[9:10], new[11:12])
        rows = spliced(recv[r, 0:span, :].astype(F32), first, second, lengths[r])
        out[r] = conv(rows, taps)
        return carry

    lax.fori_loop(0, prompts, one, 0, unroll=4)


def before_kernel(
    lengths, bias, decay, skip, taps_ref, hidden, step, u_ref, tail_ref, head_ref, dt_ref, sum_ref
):
    prompts, span, columns = hidden.shape
    local_heads = step.shape[0]
    me = lax.axis_index(AXES)
    taps = taps_ref[:, pl.ds(pl.multiple_of(me * columns, LANES), columns)].astype(F32)

    def widths(r, lens):
        return jnp.where(iota((prompts, LANES), 0) == r, lengths[r], lens)

    lens = lax.fori_loop(0, prompts, widths, jnp.zeros((prompts, LANES), jnp.int32), unroll=4)
    lane = iota((prompts, LANES), 1)
    for h in range(local_heads):
        raw = jnp.concatenate([step[h], jnp.zeros((prompts, LANES - span), F32)], axis=1)
        size = jnp.where(lane < lens, softplus(raw + bias[me * local_heads + h]), 0.0)
        total = size * -jnp.exp(jnp.full((1, LANES), decay[me * local_heads + h], F32))
        shift = 1
        while shift < span:
            total = total + jnp.where(lane >= shift, pltpu.roll(total, shift, 1), 0.0)
            shift *= 2
        dt_ref[h] = size
        sum_ref[h] = jnp.where(lane < span, total, total[:, span - 1 : span])
    place = iota((span, columns), 0)
    head_of = iota((1, columns), 1) // (columns // local_heads)
    rows = [jnp.zeros((1, columns), F32)] * 3
    for h in range(local_heads):
        given = (skip[me * local_heads + h], bias[me * local_heads + h], decay[me * local_heads + h])
        rows = [jnp.where(head_of == h, x, row) for x, row in zip(given, rows)]
    rows[2] = -jnp.exp(rows[2])
    head_ref[...] = jnp.concatenate([*rows, jnp.zeros((5, columns), F32)], axis=0)

    def one(r, carry):
        raw = hidden[r].astype(F32)
        for j in range(CONVK - 1):
            tail_ref[j, pl.ds(r, 1), :] = jnp.sum(
                jnp.where(place == lengths[r] - 3 + j, raw, 0.0), axis=0, keepdims=True
            )
        longer = jnp.concatenate([raw, jnp.zeros((8, columns), F32)], axis=0)
        u_ref[r] = conv(longer, taps)[0:span]
        return carry

    lax.fori_loop(0, prompts, one, 0, unroll=2)


def main_kernel(
    owners,
    lengths,
    taps_ref,
    mine,
    other,
    new_ref,
    gate,
    u_ref,
    tail_ref,
    consts,
    dt_given,
    sum_given,
    gated_ref,
    fin_out,
    fin,
    count,
    rank_ref,
    tokens,
    rows_ref,
    dt_ref,
    sum_ref,
):
    prompts, span, columns = gate.shape
    local_heads = dt_given.shape[0]
    head_size = columns // local_heads
    ranks(owners, count, rank_ref)
    me = lax.axis_index(AXES)
    is_b = lax.rem(me, 2) == 0
    taps = taps_ref[:, pl.ds(pl.multiple_of(me * columns, LANES), columns)].astype(F32)
    fin[...] = jnp.zeros_like(fin)

    def fetch(r, carry):
        new = new_ref[owners[r]].astype(F32)
        is_first = rank_ref[r] == 0
        for i in range(2):
            tokens[i, pl.ds(r, 1), :] = jnp.where(is_first, new[12 + i : 13 + i], new[14 + i : 15 + i])
            low = jnp.where(is_first, new[i : i + 1], new[2 + i : 3 + i])
            high = jnp.where(is_first, new[4 + i : 5 + i], new[6 + i : 7 + i])
            rows_ref[i, pl.ds(r, 1), :] = jnp.concatenate([low, high], axis=1)
        return carry

    lax.fori_loop(0, prompts, fetch, 0, unroll=4)
    raws = [tail_ref[0], tail_ref[1], tail_ref[2], rows_ref[0], rows_ref[1]]
    for i in range(2):
        total = sum(raws[i + k] * taps[k : k + 1] for k in range(CONVK))
        rows_ref[i] = silu(total).astype(BF16).astype(F32)

    def widths(r, lens):
        return jnp.where(iota((prompts, LANES), 0) == r, lengths[r], lens)

    lens = lax.fori_loop(0, prompts, widths, jnp.zeros((prompts, LANES), jnp.int32))
    lane = iota((prompts, LANES), 1)
    news = []
    for i in range(2):
        raw = tokens[i]
        news.append(raw + pltpu.roll(raw, LANES - 32, 1) + pltpu.roll(raw, LANES - 64, 1))
    for h in range(local_heads):
        at = slice(h * head_size, h * head_size + 1)
        rate = consts[2:3, at]
        first, second = [softplus(x[:, h : h + 1] + consts[1:2, at]) for x in news]
        dt_ref[:, h, :] = jnp.where(
            lane == lens, first, jnp.where(lane == lens + 1, second, dt_given[h])
        )
        sum_ref[:, h, :] = (
            sum_given[h]
            + jnp.where(lane >= lens, first * rate, 0.0)
            + jnp.where(lane > lens, second * rate, 0.0)
        )

    gain = consts[0:1, :]
    heads_wide = div(iota((ROWS, columns), 1), head_size)
    place = iota((ROWS, columns), 0)
    lower = iota((ROWS, ROWS), 0) >= iota((ROWS, ROWS), 1)
    column_of = iota((span, LANES), 1)

    def one(r, squares):
        owner = owners[r]
        rank = rank_ref[r]
        length = lengths[r]
        wide = jnp.concatenate(
            [u_ref[r].astype(F32), jnp.zeros((ROWS - span, columns), F32)], axis=0
        )
        wide = jnp.where(
            place == length,
            rows_ref[0, pl.ds(r, 1), :],
            jnp.where(place == length + 1, rows_ref[1, pl.ds(r, 1), :], wide),
        )
        u = wide.astype(BF16)
        here, there = mine[r], other[r]
        b_rows = jnp.where(is_b, here, there)
        c_rows = jnp.where(is_b, there, here)
        scores = lax.dot_general(
            c_rows, b_rows, (((1,), (1,)), ((), ())), preferred_element_type=F32
        )
        sums = sum_ref[r]
        sizes = dt_ref[r]
        turned = sums.T
        out = gain * wide
        for h in range(local_heads):
            gap = turned[:ROWS, h : h + 1] - sums[h : h + 1, :ROWS]
            mix = jnp.where(lower, scores * jnp.exp(gap) * sizes[h : h + 1, :ROWS], 0.0)
            only = jnp.where(heads_wide == h, u, jnp.zeros((), BF16))
            out = out + jnp.dot(mix.astype(BF16), only, preferred_element_type=F32)
        for i in range(2):
            row = jnp.sum(jnp.where(place == length + i, out, 0.0), axis=0, keepdims=True)
            for half in range(2):
                fin[owner, pl.ds(4 * half + 2 * rank + i, 1), :] = row[
                    :, half * LANES : (half + 1) * LANES
                ]
        gated = out[:span] * silu(gate[r].astype(F32))
        gated_ref[r] = gated
        square = jnp.sum(gated * gated, axis=1, keepdims=True)
        return jnp.where(column_of == r, square, squares)

    squares = lax.fori_loop(0, prompts, one, jnp.zeros((span, LANES), F32), unroll=4)
    turned = squares.T
    half = prompts // 2
    packed = jnp.concatenate([turned[0:half, :], turned[half:prompts, :]], axis=1)

    high = packed.astype(BF16).astype(F32)
    split = (high, packed - high)

    def spread(d, carry):
        fin_out[d] = jnp.concatenate([*split, fin[d]], axis=0).astype(BF16)
        return carry

    lax.fori_loop(0, fin.shape[0], spread, 0, unroll=4)


def slot_facts(owners, lengths, slots):
    me = lax.axis_index(AXES)

    def one(r, found):
        is_mine = owners[r] == me
        seen = found[-1]
        lens = [
            jnp.where(is_mine & (seen == k), lengths[r], found[k]) for k in range(slots)
        ]
        return (*lens, seen + is_mine.astype(jnp.int32))

    zero = jnp.int32(0)
    return lax.fori_loop(0, owners.shape[0], one, (zero,) * (slots + 1), unroll=8)[:slots]


def cache_kernel(owners, lengths, pages, query, cache_new, crossed, *refs):
    straight, (pool, attended, rows_ref) = refs[:-3], refs[-3:]
    slots = query.shape[0]
    steps = query.shape[1]
    chips = len(straight)
    sources = 2 * chips
    width = pool.shape[2]
    parts = width // LANES
    span = pool.shape[0] // slots * BLK
    each = crossed.shape[1] // parts
    local = each // slots
    lens = slot_facts(owners, lengths, slots)
    keys = sources * each
    key = iota((1, keys), 1)
    block_of = div(key, each)
    apart = mod(block_of, chips) * 2 + div(block_of, chips)
    slot_of = div(mod(key, each), local)
    at = (apart ^ lax.axis_index(AXES)) * local + mod(key, local)
    wanted = jnp.where(at < jnp.where(slot_of == 0, lens[0], lens[1]), slot_of * span + at, -1)
    order = jnp.where(iota((slots * span, keys), 0) == wanted, 1.0, 0.0).astype(BF16)
    ask = jnp.concatenate([query[k].astype(F32) for k in range(slots)], axis=0)
    fresh = jnp.concatenate([cache_new[k].astype(F32) for k in range(slots)], axis=0)
    fresh = jnp.concatenate([fresh, jnp.zeros_like(fresh)], axis=0)
    per = query.shape[2] // (KVH * KVD)
    pairs = slots * steps
    count = per * pairs
    row = iota((count, 1), 0)
    ask_slot, ask_step = div(mod(row, pairs), steps), mod(row, steps)
    key = iota((1, slots * span), 1)
    is_live = mod(key, span) < jnp.where(div(key, span) == 0, lens[0], lens[1])
    live = ask_slot == jnp.where(is_live, div(key, span), -1)
    key = iota((1, 2 * pairs), 1)
    new_live = (ask_slot == jnp.where(key < pairs, div(key, steps), -1)) & (
        mod(key, steps) <= ask_step
    )
    filled = jnp.where(ask_slot == 0, lens[0], lens[1]) > 0

    for c in range(parts):
        strip = slice(c * each, (c + 1) * each)
        block = jnp.concatenate(
            [ref[0, strip, :].astype(F32) for ref in straight]
            + [crossed[m, strip, :].astype(F32) for m in range(chips)],
            axis=0,
        ).astype(BF16)
        rows_ref[:, c * LANES : (c + 1) * LANES] = jnp.dot(
            order, block, preferred_element_type=F32
        ).astype(BF16)
    blocks = span // BLK
    for k in range(slots):
        for b in range(blocks):
            pool[pages[0, k * blocks + b]] = rows_ref[
                k * span + b * BLK : k * span + (b + 1) * BLK, :
            ]
    contract = (((1,), (1,)), ((), ()))
    answers = []
    for c in range(KVH):
        asked = jnp.concatenate(
            [ask[:, (c * per + g) * KVD : (c * per + g + 1) * KVD] for g in range(per)], axis=0
        ).astype(BF16)
        own = slice(c * KVD, (c + 1) * KVD)
        values = slice((KVH + c) * KVD, (KVH + c + 1) * KVD)
        old = lax.dot_general(asked, rows_ref[:, own], contract, preferred_element_type=F32)
        recent = lax.dot_general(
            asked, fresh[:, own].astype(BF16), contract, preferred_element_type=F32
        )
        old = jnp.where(live, old * KVD ** (-0.5), -jnp.inf)
        recent = jnp.where(new_live, recent * KVD ** (-0.5), -jnp.inf)
        peak = jnp.maximum(
            jnp.max(old, axis=1, keepdims=True), jnp.max(recent, axis=1, keepdims=True)
        )
        old = jnp.exp(old - peak)
        recent = jnp.exp(recent - peak)
        total = jnp.sum(old, axis=1, keepdims=True) + jnp.sum(recent, axis=1, keepdims=True)
        got = jnp.dot(
            (old / total).astype(BF16), rows_ref[:, values], preferred_element_type=F32
        ) + jnp.dot(
            (recent / total).astype(BF16),
            fresh[:, values].astype(BF16),
            preferred_element_type=F32,
        )
        got = jnp.where(filled, got, 0.0)
        answers += [got[g * pairs : (g + 1) * pairs] for g in range(per)]
    whole = jnp.concatenate(answers, axis=1)
    for k in range(slots):
        attended[k] = whole[k * steps : (k + 1) * steps].astype(BF16)


def final_kernel(owners, lengths, gain_ref, fin, gated, new_gate, prefill, mixer):
    prompts, span, columns = gated.shape
    slots = new_gate.shape[0]
    steps = new_gate.shape[1]
    sources = fin.shape[0]
    width = new_gate.shape[2]
    half = prompts // 2
    me = lax.axis_index(AXES)
    blocks = [fin[s].astype(F32) for s in range(sources)]
    total = sum(x[half : 2 * half] for x in blocks) + sum(x[0:half] for x in blocks)
    scale = lax.rsqrt(total / width + EPS).T
    gain = gain_ref[:, pl.ds(pl.multiple_of(me * columns, LANES), columns)]
    place = iota((span, columns), 0)
    for r in range(prompts):
        low = 0 if r < half else span
        column = scale[low : low + span, r % half : r % half + 1]
        rows = gated[r] * column * gain
        prefill[r] = jnp.where(place < lengths[r], rows, 0.0).astype(BF16)
    lens = slot_facts(owners, lengths, slots)
    read = jnp.concatenate(
        [
            block[2 * half + pairs : 2 * half + pairs + 4]
            for block in blocks
            for pairs in (0, 4)
        ],
        axis=1,
    )
    gates = jnp.concatenate([new_gate[k].astype(F32) for k in range(slots)], axis=0)
    out = read * silu(gates)
    mean = jnp.mean(out * out, axis=1, keepdims=True)
    out = out * lax.rsqrt(mean + EPS) * gain_ref[...]
    slot_of = div(iota((out.shape[0], 1), 0), steps)
    out = jnp.where(jnp.where(slot_of == 0, lens[0], lens[1]) > 0, out, 0.0)
    for k in range(slots):
        mixer[k] = out[k * steps : (k + 1) * steps].astype(BF16)


def local(
    hidden_pre,
    coeff_pre,
    gate_pre,
    step_raw,
    cache_rows,
    lengths,
    owners,
    page_table,
    conv_hidden,
    conv_coeff,
    step_bias,
    decay_log,
    skip_gain,
    norm_gain,
    new_hidden,
    new_coeff,
    new_gate,
    new_step,
    new_query,
    new_cache,
):
    devices = lax.axis_size(AXES)
    prompts, span, columns = hidden_pre.shape
    slots = new_hidden.shape[0]
    local_heads = step_raw.shape[0]
    cache_width = cache_rows.shape[2]
    kept_rows = slots * cache_rows.shape[1] * cache_width // LANES
    per_owner = pltpu.SMEM((devices,), jnp.int32)
    per_prompt = pltpu.SMEM((prompts,), jnp.int32)

    owners = owners[:, 0]
    send = pl.pallas_call(
        pack_kernel,
        out_shape=jax.ShapeDtypeStruct((devices, span + NEW, LANES), BF16),
        in_specs=[ANY, ANY, ANY, ANY],
        out_specs=VMEM,
        scratch_shapes=[
            pltpu.VMEM(new_hidden.shape, BF16),
            pltpu.VMEM(new_coeff.shape, BF16),
            pltpu.VMEM(new_step.shape, F32),
            pltpu.SemaphoreType.DMA((3 + devices,)),
        ],
        name="pack",
    )(coeff_pre, new_hidden, new_coeff, new_step)
    recv = lax.all_to_all(send, AXES, split_axis=0, concat_axis=0, tiled=True)
    chips = devices // 2
    kept = pl.pallas_call(
        pack_cache_kernel,
        out_shape=(jax.ShapeDtypeStruct((2, kept_rows, LANES), BF16),) * chips,
        in_specs=[SMEM, VMEM],
        out_specs=(VMEM,) * chips,
        scratch_shapes=[per_owner, pltpu.SMEM((devices * slots,), jnp.int32)],
        compiler_params=PARAMS,
        cost_estimate=cost(3),
        name="pack_cache",
    )(owners, cache_rows)
    kept = [kept[0]] + [
        lax.ppermute(kept[m], "tensor", [(i, i ^ m) for i in range(chips)])
        for m in range(1, chips)
    ]
    before = pl.pallas_call(
        before_kernel,
        out_shape=(
            jax.ShapeDtypeStruct((prompts, span, columns), BF16),
            jax.ShapeDtypeStruct((CONVK - 1, prompts, columns), F32),
            jax.ShapeDtypeStruct((8, columns), F32),
            jax.ShapeDtypeStruct((local_heads, prompts, LANES), F32),
            jax.ShapeDtypeStruct((local_heads, prompts, LANES), F32),
        ),
        in_specs=[SMEM] * 4 + [VMEM] * 3,
        out_specs=(VMEM,) * 5,
        compiler_params=PARAMS,
        cost_estimate=cost(4),
        name="before",
    )(lengths, step_bias, decay_log, skip_gain, conv_hidden, hidden_pre, step_raw)
    early = (1, 3, 6)
    recv, sums, *held = lax.optimization_barrier(
        (recv, before[-1], *(kept[m] for m in early))
    )
    before = (*before[:-1], sums)
    for m, block in zip(early, held):
        kept[m] = block

    mine = pl.pallas_call(
        coeff_kernel,
        grid=(1,),
        out_shape=jax.ShapeDtypeStruct((prompts, ROWS, LANES), BF16),
        in_specs=[
            SMEM,
            SMEM,
            VMEM,
            pl.BlockSpec((devices, span + NEW, LANES), lambda i: (0, 0, 0)),
        ],
        out_specs=VMEM,
        scratch_shapes=[per_owner, per_prompt],
        compiler_params=PARAMS,
        cost_estimate=cost(2),
        name="coeff",
    )(owners, lengths, conv_coeff, recv)
    other = lax.ppermute(mine, "side", [(0, 1), (1, 0)])

    new_block = span // NEW
    gated, fin = pl.pallas_call(
        main_kernel,
        grid=(1,),
        out_shape=(
            jax.ShapeDtypeStruct((prompts, span, columns), F32),
            jax.ShapeDtypeStruct((devices, prompts + 8, LANES), BF16),
        ),
        in_specs=[SMEM] * 2
        + [VMEM] * 3
        + [pl.BlockSpec((devices, NEW, LANES), lambda i: (0, new_block, 0))]
        + [VMEM] * 6,
        out_specs=(VMEM, VMEM),
        scratch_shapes=[
            pltpu.VMEM((devices, 8, LANES), F32),
            per_owner,
            per_prompt,
            pltpu.VMEM((2, prompts, LANES), F32),
            pltpu.VMEM((2, prompts, columns), F32),
            pltpu.VMEM((prompts, 8, LANES), F32),
            pltpu.VMEM((prompts, 8, LANES), F32),
        ],
        compiler_params=PARAMS,
        cost_estimate=cost(10),
        name="main",
    )(
        owners,
        lengths,
        conv_hidden,
        mine,
        other,
        recv,
        gate_pre,
        *before,
    )
    fin, *kept = lax.optimization_barrier((fin, *kept))
    crossed = pl.pallas_call(
        stack_kernel,
        out_shape=jax.ShapeDtypeStruct((chips, kept_rows, LANES), BF16),
        in_specs=[VMEM] * chips,
        out_specs=VMEM,
        compiler_params=PARAMS,
        cost_estimate=cost(1),
        name="stack",
    )(*kept)
    crossed = lax.ppermute(crossed, "side", [(0, 1), (1, 0)])
    fin_got = lax.all_to_all(fin, AXES, split_axis=0, concat_axis=0, tiled=True)

    cache_pool, decode_attention = pl.pallas_call(
        cache_kernel,
        out_shape=(
            jax.ShapeDtypeStruct((page_table.shape[1], BLK, cache_width), BF16),
            jax.ShapeDtypeStruct(new_query.shape, BF16),
        ),
        in_specs=[SMEM] * 3 + [VMEM] * (3 + chips),
        out_specs=(VMEM, VMEM),
        scratch_shapes=[pltpu.VMEM((slots * span, cache_width), BF16)],
        compiler_params=PARAMS,
        cost_estimate=cost(5),
        name="cache",
    )(owners, lengths, page_table, new_query, new_cache, crossed, *kept)

    fin_got, cache_pool = lax.optimization_barrier((fin_got, cache_pool))
    prefill_out, decode_mixer = pl.pallas_call(
        final_kernel,
        out_shape=(
            jax.ShapeDtypeStruct(hidden_pre.shape, BF16),
            jax.ShapeDtypeStruct(new_gate.shape, BF16),
        ),
        in_specs=[SMEM, SMEM, VMEM, VMEM, VMEM, VMEM],
        out_specs=(VMEM, VMEM),
        compiler_params=PARAMS,
        name="final",
    )(owners, lengths, norm_gain.reshape(1, -1), fin_got, gated, new_gate)
    return (prefill_out, cache_pool, decode_mixer, decode_attention)


def solution(mesh):
    own = P(("group", "tensor", "side"), None, None)
    placed = (
        P("group", None, ("tensor", "side")),
        own,
        P("group", None, ("tensor", "side")),
        P(("tensor", "side"), "group", None),
        P("group", ("tensor", "side"), None),
        P("group"),
        P("group", None),
        P(("group", "tensor", "side"), None),
        P(),
        P(),
        P(),
        P(),
        P(),
        P(),
        own,
        own,
        own,
        own,
        own,
        own,
    )
    return jax.shard_map(
        local,
        mesh=mesh,
        in_specs=placed,
        out_specs=(P("group", None, ("tensor", "side")), own, own, own),
        check_vma=False,
    )
```

```python
import jax
import jax.numpy as jnp
from jax import lax
from jax.experimental import pallas as pl
from jax.experimental.pallas import tpu as pltpu
from jax.sharding import PartitionSpec as P

GROUPS = 8
CONVK = 4
KVH = 8
KVD = 128
BLK = 16
LANES = 128
ROWS = 80
NEW = 16
EPS = 1e-05
AXES = ("tensor", "side")
F32 = jnp.float32
BF16 = jnp.bfloat16

SMEM = pl.BlockSpec(memory_space=pltpu.SMEM)
VMEM = pl.BlockSpec(memory_space=pltpu.VMEM)
ANY = pl.BlockSpec(memory_space=pl.ANY)
PARAMS = pltpu.CompilerParams(vmem_limit_bytes=48 * 1024 * 1024)


def cost(microseconds):
    return pl.CostEstimate(flops=0, bytes_accessed=microseconds * 3_500_000, transcendentals=0)


def iota(shape, dim):
    return lax.broadcasted_iota(jnp.int32, shape, dim)


def div(x, n):
    return x >> (n.bit_length() - 1) if n & (n - 1) == 0 else x // n


def mod(x, n):
    return x & (n - 1) if n & (n - 1) == 0 else lax.rem(x, n)


def softplus(x):
    return jnp.maximum(x, 0.0) + jnp.log1p(jnp.exp(-jnp.abs(x)))


def silu(x):
    return x / (1.0 + jnp.exp(-x))


def ranks(owners, count, rank_ref):
    def clear(d, carry):
        count[d] = 0
        return carry

    lax.fori_loop(0, count.shape[0], clear, 0)

    def one(r, carry):
        owner = owners[r]
        rank = count[owner]
        rank_ref[r] = rank
        count[owner] = rank + 1
        return carry

    lax.fori_loop(0, owners.shape[0], one, 0)


def pack_kernel(coeff, hidden_in, coeff_new_in, step_in, send, hidden, coeff_new, step_new, sems):
    devices = send.shape[0]
    slots = hidden.shape[0]
    group_devs = devices // GROUPS
    span = coeff.shape[1]
    news = [
        pltpu.make_async_copy(a, b, sems.at[i])
        for i, (a, b) in enumerate(
            ((hidden_in, hidden), (coeff_new_in, coeff_new), (step_in, step_new))
        )
    ]

    def start_of(d):
        return pl.multiple_of((d // group_devs * 2 + lax.rem(d, 2)) * LANES, LANES)

    def piece(d):
        return pltpu.make_async_copy(
            coeff.at[0, :, pl.ds(start_of(d), LANES)],
            send.at[d, pl.ds(0, span), :],
            sems.at[3 + d],
        )

    for copy in news:
        copy.start()

    def begin(d, carry):
        piece(d).start()
        return carry

    lax.fori_loop(0, devices, begin, 0)
    for copy in news:
        copy.wait()

    heads = step_new.shape[2]
    steps = jnp.concatenate([step_new[k] for k in range(slots)], axis=0)
    if heads < LANES:
        steps = jnp.concatenate(
            [steps, jnp.zeros((steps.shape[0], LANES - heads), F32)], axis=1
        )
    steps = jnp.concatenate([steps, jnp.zeros_like(steps)], axis=0)
    padded = steps.shape[1]
    lane = iota((8, LANES), 1)

    def one(d, carry):
        own = pl.multiple_of(d * 2 * LANES, 2 * LANES)
        rows = jnp.concatenate(
            [hidden[k, :, pl.ds(own, 2 * LANES)].astype(F32) for k in range(slots)], axis=0
        )
        tokens = jnp.concatenate(
            [coeff_new[k, :, pl.ds(start_of(d), LANES)].astype(F32) for k in range(slots)], axis=0
        )
        mine = pltpu.roll(steps, lax.rem(padded - d * 4, padded), 1)[:, :LANES]
        high = mine.astype(BF16).astype(F32)
        rest = mine - high
        middle = rest.astype(BF16).astype(F32)
        low = rest - middle
        split = jnp.where(
            lane < 32, high, jnp.where(lane < 64, pltpu.roll(middle, 32, 1), pltpu.roll(low, 64, 1))
        )
        block = jnp.concatenate([rows[:, :LANES], rows[:, LANES:], tokens, split[0:4]], axis=0)
        send[d, span : span + NEW, :] = block.astype(BF16)
        return carry

    lax.fori_loop(0, devices, one, 0, unroll=8)

    def end(d, carry):
        piece(d).wait()
        return carry

    lax.fori_loop(0, devices, end, 0)


def pack_cache_kernel(owners, cache, *refs):
    outs, (count, source) = refs[:-2], refs[-2:]
    devices = count.shape[0]
    slots = source.shape[0] // devices
    width = cache.shape[2]

    def clear(d, carry):
        count[d] = 0
        for k in range(slots):
            source[d * slots + k] = 0
        return carry

    lax.fori_loop(0, devices, clear, 0, unroll=4)

    def place(r, carry):
        owner = owners[r]
        rank = count[owner]
        source[owner * slots + rank] = r
        count[owner] = rank + 1
        return carry

    lax.fori_loop(0, owners.shape[0], place, 0, unroll=4)
    me = lax.axis_index(AXES)
    for m, out in enumerate(outs):
        for x in range(2):
            d = me ^ (2 * m + x)
            kept = jnp.concatenate(
                [cache[source[d * slots + k]].astype(F32) for k in range(slots)], axis=0
            )
            kept = jnp.concatenate(
                [kept[:, c * LANES : (c + 1) * LANES] for c in range(width // LANES)], axis=0
            )
            out[x] = kept.astype(BF16)


def stack_kernel(*refs):
    for m, ref in enumerate(refs[:-1]):
        refs[-1][m] = ref[1]


def spliced(rows, first, second, length):
    columns = rows.shape[1]
    rows = jnp.concatenate([rows, jnp.zeros((ROWS - rows.shape[0], columns), F32)], axis=0)
    place = iota((ROWS, columns), 0)
    return jnp.where(place == length, first, jnp.where(place == length + 1, second, rows))


def conv(rows, taps):
    total = pltpu.roll(rows, 3, 0) * taps[0:1]
    total = total + pltpu.roll(rows, 2, 0) * taps[1:2]
    total = total + pltpu.roll(rows, 1, 0) * taps[2:3]
    total = total + rows * taps[3:4]
    return silu(total).astype(BF16)


def coeff_kernel(owners, lengths, taps_ref, recv, out, count, rank_ref):
    prompts = out.shape[0]
    span = recv.shape[1] - NEW
    devices = recv.shape[0]
    group_devs = devices // GROUPS
    ranks(owners, count, rank_ref)
    me = lax.axis_index(AXES)
    start = pl.multiple_of((me // group_devs * 2 + lax.rem(me, 2)) * LANES, LANES)
    taps = taps_ref[:, pl.ds(start, LANES)].astype(F32)

    def one(r, carry):
        new = recv[owners[r], span : span + NEW, :].astype(F32)
        is_first = rank_ref[r] == 0
        first = jnp.where(is_first, new[8:9], new[10:11])
        second = jnp.where(is_first, new[9:10], new[11:12])
        rows = spliced(recv[r, 0:span, :].astype(F32), first, second, lengths[r])
        out[r] = conv(rows, taps)
        return carry

    lax.fori_loop(0, prompts, one, 0, unroll=8)


def before_kernel(
    lengths, bias, decay, skip, taps_ref, hidden, step, u_ref, tail_ref, head_ref, dt_ref, sum_ref
):
    prompts, span, columns = hidden.shape
    local_heads = step.shape[0]
    me = lax.axis_index(AXES)
    taps = taps_ref[:, pl.ds(pl.multiple_of(me * columns, LANES), columns)].astype(F32)

    def widths(r, lens):
        return jnp.where(iota((prompts, LANES), 0) == r, lengths[r], lens)

    lens = lax.fori_loop(0, prompts, widths, jnp.zeros((prompts, LANES), jnp.int32), unroll=4)
    lane = iota((prompts, LANES), 1)
    for h in range(local_heads):
        raw = jnp.concatenate([step[h], jnp.zeros((prompts, LANES - span), F32)], axis=1)
        size = jnp.where(lane < lens, softplus(raw + bias[me * local_heads + h]), 0.0)
        total = size * -jnp.exp(jnp.full((1, LANES), decay[me * local_heads + h], F32))
        shift = 1
        while shift < span:
            total = total + jnp.where(lane >= shift, pltpu.roll(total, shift, 1), 0.0)
            shift *= 2
        dt_ref[h] = size
        sum_ref[h] = jnp.where(lane < span, total, total[:, span - 1 : span])
    place = iota((span, columns), 0)
    head_of = iota((1, columns), 1) // (columns // local_heads)
    rows = [jnp.zeros((1, columns), F32)] * 3
    for h in range(local_heads):
        given = (skip[me * local_heads + h], bias[me * local_heads + h], decay[me * local_heads + h])
        rows = [jnp.where(head_of == h, x, row) for x, row in zip(given, rows)]
    rows[2] = -jnp.exp(rows[2])
    head_ref[...] = jnp.concatenate([*rows, jnp.zeros((5, columns), F32)], axis=0)

    def one(r, carry):
        raw = hidden[r].astype(F32)
        for j in range(CONVK - 1):
            tail_ref[j, pl.ds(r, 1), :] = jnp.sum(
                jnp.where(place == lengths[r] - 3 + j, raw, 0.0), axis=0, keepdims=True
            )
        longer = jnp.concatenate([raw, jnp.zeros((8, columns), F32)], axis=0)
        u_ref[r] = conv(longer, taps)[0:span]
        return carry

    lax.fori_loop(0, prompts, one, 0, unroll=2)


def main_kernel(
    owners,
    lengths,
    taps_ref,
    mine,
    other,
    new_ref,
    gate,
    u_ref,
    tail_ref,
    consts,
    dt_given,
    sum_given,
    gated_ref,
    fin_out,
    fin,
    count,
    rank_ref,
    tokens,
    rows_ref,
    dt_ref,
    sum_ref,
):
    prompts, span, columns = gate.shape
    local_heads = dt_given.shape[0]
    head_size = columns // local_heads
    ranks(owners, count, rank_ref)
    me = lax.axis_index(AXES)
    is_b = lax.rem(me, 2) == 0
    taps = taps_ref[:, pl.ds(pl.multiple_of(me * columns, LANES), columns)].astype(F32)
    fin[...] = jnp.zeros_like(fin)

    def fetch(r, carry):
        new = new_ref[owners[r]].astype(F32)
        is_first = rank_ref[r] == 0
        for i in range(2):
            tokens[i, pl.ds(r, 1), :] = jnp.where(is_first, new[12 + i : 13 + i], new[14 + i : 15 + i])
            low = jnp.where(is_first, new[i : i + 1], new[2 + i : 3 + i])
            high = jnp.where(is_first, new[4 + i : 5 + i], new[6 + i : 7 + i])
            rows_ref[i, pl.ds(r, 1), :] = jnp.concatenate([low, high], axis=1)
        return carry

    lax.fori_loop(0, prompts, fetch, 0, unroll=8)
    raws = [tail_ref[0], tail_ref[1], tail_ref[2], rows_ref[0], rows_ref[1]]
    for i in range(2):
        total = sum(raws[i + k] * taps[k : k + 1] for k in range(CONVK))
        rows_ref[i] = silu(total).astype(BF16).astype(F32)

    def widths(r, lens):
        return jnp.where(iota((prompts, LANES), 0) == r, lengths[r], lens)

    lens = lax.fori_loop(0, prompts, widths, jnp.zeros((prompts, LANES), jnp.int32))
    lane = iota((prompts, LANES), 1)
    news = []
    for i in range(2):
        raw = tokens[i]
        news.append(raw + pltpu.roll(raw, LANES - 32, 1) + pltpu.roll(raw, LANES - 64, 1))
    for h in range(local_heads):
        at = slice(h * head_size, h * head_size + 1)
        rate = consts[2:3, at]
        first, second = [softplus(x[:, h : h + 1] + consts[1:2, at]) for x in news]
        dt_ref[:, h, :] = jnp.where(
            lane == lens, first, jnp.where(lane == lens + 1, second, dt_given[h])
        )
        sum_ref[:, h, :] = (
            sum_given[h]
            + jnp.where(lane >= lens, first * rate, 0.0)
            + jnp.where(lane > lens, second * rate, 0.0)
        )

    gain = consts[0:1, :]
    heads_wide = div(iota((ROWS, columns), 1), head_size)
    place = iota((ROWS, columns), 0)
    lower = iota((ROWS, ROWS), 0) >= iota((ROWS, ROWS), 1)
    column_of = iota((span, LANES), 1)

    def one(r, squares):
        owner = owners[r]
        rank = rank_ref[r]
        length = lengths[r]
        wide = jnp.concatenate(
            [u_ref[r].astype(F32), jnp.zeros((ROWS - span, columns), F32)], axis=0
        )
        wide = jnp.where(
            place == length,
            rows_ref[0, pl.ds(r, 1), :],
            jnp.where(place == length + 1, rows_ref[1, pl.ds(r, 1), :], wide),
        )
        u = wide.astype(BF16)
        here, there = mine[r], other[r]
        b_rows = jnp.where(is_b, here, there)
        c_rows = jnp.where(is_b, there, here)
        scores = lax.dot_general(
            c_rows, b_rows, (((1,), (1,)), ((), ())), preferred_element_type=F32
        )
        sums = sum_ref[r]
        sizes = dt_ref[r]
        turned = sums.T
        out = gain * wide
        for h in range(local_heads):
            gap = turned[:ROWS, h : h + 1] - sums[h : h + 1, :ROWS]
            mix = jnp.where(lower, scores * jnp.exp(gap) * sizes[h : h + 1, :ROWS], 0.0)
            only = jnp.where(heads_wide == h, u, jnp.zeros((), BF16))
            out = out + jnp.dot(mix.astype(BF16), only, preferred_element_type=F32)
        for i in range(2):
            row = jnp.sum(jnp.where(place == length + i, out, 0.0), axis=0, keepdims=True)
            for half in range(2):
                fin[owner, pl.ds(4 * half + 2 * rank + i, 1), :] = row[
                    :, half * LANES : (half + 1) * LANES
                ]
        gated = out[:span] * silu(gate[r].astype(F32))
        gated_ref[r] = gated
        square = jnp.sum(gated * gated, axis=1, keepdims=True)
        return jnp.where(column_of == r, square, squares)

    squares = lax.fori_loop(0, prompts, one, jnp.zeros((span, LANES), F32), unroll=8)
    turned = squares.T
    half = prompts // 2
    packed = jnp.concatenate([turned[0:half, :], turned[half:prompts, :]], axis=1)

    high = packed.astype(BF16).astype(F32)
    split = (high, packed - high)

    def spread(d, carry):
        fin_out[d] = jnp.concatenate([*split, fin[d]], axis=0).astype(BF16)
        return carry

    lax.fori_loop(0, fin.shape[0], spread, 0, unroll=4)


def slot_facts(owners, lengths, slots):
    me = lax.axis_index(AXES)

    def one(r, found):
        is_mine = owners[r] == me
        seen = found[-1]
        lens = [
            jnp.where(is_mine & (seen == k), lengths[r], found[k]) for k in range(slots)
        ]
        return (*lens, seen + is_mine.astype(jnp.int32))

    zero = jnp.int32(0)
    return lax.fori_loop(0, owners.shape[0], one, (zero,) * (slots + 1), unroll=8)[:slots]


def cache_kernel(owners, lengths, pages, query, cache_new, crossed, *refs):
    straight, (pool, attended, rows_ref) = refs[:-3], refs[-3:]
    slots = query.shape[0]
    steps = query.shape[1]
    chips = len(straight)
    sources = 2 * chips
    width = pool.shape[2]
    parts = width // LANES
    span = pool.shape[0] // slots * BLK
    each = crossed.shape[1] // parts
    local = each // slots
    lens = slot_facts(owners, lengths, slots)
    keys = sources * each
    key = iota((1, keys), 1)
    block_of = div(key, each)
    apart = mod(block_of, chips) * 2 + div(block_of, chips)
    slot_of = div(mod(key, each), local)
    at = (apart ^ lax.axis_index(AXES)) * local + mod(key, local)
    wanted = jnp.where(at < jnp.where(slot_of == 0, lens[0], lens[1]), slot_of * span + at, -1)
    order = jnp.where(iota((slots * span, keys), 0) == wanted, 1.0, 0.0).astype(BF16)
    ask = jnp.concatenate([query[k].astype(F32) for k in range(slots)], axis=0)
    fresh = jnp.concatenate([cache_new[k].astype(F32) for k in range(slots)], axis=0)
    fresh = jnp.concatenate([fresh, jnp.zeros_like(fresh)], axis=0)
    per = query.shape[2] // (KVH * KVD)
    pairs = slots * steps
    count = per * pairs
    row = iota((count, 1), 0)
    ask_slot, ask_step = div(mod(row, pairs), steps), mod(row, steps)
    key = iota((1, slots * span), 1)
    is_live = mod(key, span) < jnp.where(div(key, span) == 0, lens[0], lens[1])
    live = ask_slot == jnp.where(is_live, div(key, span), -1)
    key = iota((1, 2 * pairs), 1)
    new_live = (ask_slot == jnp.where(key < pairs, div(key, steps), -1)) & (
        mod(key, steps) <= ask_step
    )
    filled = jnp.where(ask_slot == 0, lens[0], lens[1]) > 0

    for c in range(parts):
        strip = slice(c * each, (c + 1) * each)
        block = jnp.concatenate(
            [ref[0, strip, :].astype(F32) for ref in straight]
            + [crossed[m, strip, :].astype(F32) for m in range(chips)],
            axis=0,
        ).astype(BF16)
        rows_ref[:, c * LANES : (c + 1) * LANES] = jnp.dot(
            order, block, preferred_element_type=F32
        ).astype(BF16)
    blocks = span // BLK
    for k in range(slots):
        for b in range(blocks):
            pool[pages[0, k * blocks + b]] = rows_ref[
                k * span + b * BLK : k * span + (b + 1) * BLK, :
            ]
    contract = (((1,), (1,)), ((), ()))
    answers = []
    for c in range(KVH):
        asked = jnp.concatenate(
            [ask[:, (c * per + g) * KVD : (c * per + g + 1) * KVD] for g in range(per)], axis=0
        ).astype(BF16)
        own = slice(c * KVD, (c + 1) * KVD)
        values = slice((KVH + c) * KVD, (KVH + c + 1) * KVD)
        old = lax.dot_general(asked, rows_ref[:, own], contract, preferred_element_type=F32)
        recent = lax.dot_general(
            asked, fresh[:, own].astype(BF16), contract, preferred_element_type=F32
        )
        old = jnp.where(live, old * KVD ** (-0.5), -jnp.inf)
        recent = jnp.where(new_live, recent * KVD ** (-0.5), -jnp.inf)
        peak = jnp.maximum(
            jnp.max(old, axis=1, keepdims=True), jnp.max(recent, axis=1, keepdims=True)
        )
        old = jnp.exp(old - peak)
        recent = jnp.exp(recent - peak)
        total = jnp.sum(old, axis=1, keepdims=True) + jnp.sum(recent, axis=1, keepdims=True)
        got = jnp.dot(
            (old / total).astype(BF16), rows_ref[:, values], preferred_element_type=F32
        ) + jnp.dot(
            (recent / total).astype(BF16),
            fresh[:, values].astype(BF16),
            preferred_element_type=F32,
        )
        got = jnp.where(filled, got, 0.0)
        answers += [got[g * pairs : (g + 1) * pairs] for g in range(per)]
    whole = jnp.concatenate(answers, axis=1)
    for k in range(slots):
        attended[k] = whole[k * steps : (k + 1) * steps].astype(BF16)


def final_kernel(owners, lengths, gain_ref, fin, gated, new_gate, prefill, mixer):
    prompts, span, columns = gated.shape
    slots = new_gate.shape[0]
    steps = new_gate.shape[1]
    sources = fin.shape[0]
    width = new_gate.shape[2]
    half = prompts // 2
    me = lax.axis_index(AXES)
    blocks = [fin[s].astype(F32) for s in range(sources)]
    total = sum(x[half : 2 * half] for x in blocks) + sum(x[0:half] for x in blocks)
    scale = lax.rsqrt(total / width + EPS).T
    gain = gain_ref[:, pl.ds(pl.multiple_of(me * columns, LANES), columns)]
    place = iota((span, columns), 0)
    for r in range(prompts):
        low = 0 if r < half else span
        column = scale[low : low + span, r % half : r % half + 1]
        rows = gated[r] * column * gain
        prefill[r] = jnp.where(place < lengths[r], rows, 0.0).astype(BF16)
    lens = slot_facts(owners, lengths, slots)
    read = jnp.concatenate(
        [
            block[2 * half + pairs : 2 * half + pairs + 4]
            for block in blocks
            for pairs in (0, 4)
        ],
        axis=1,
    )
    gates = jnp.concatenate([new_gate[k].astype(F32) for k in range(slots)], axis=0)
    out = read * silu(gates)
    mean = jnp.mean(out * out, axis=1, keepdims=True)
    out = out * lax.rsqrt(mean + EPS) * gain_ref[...]
    slot_of = div(iota((out.shape[0], 1), 0), steps)
    out = jnp.where(jnp.where(slot_of == 0, lens[0], lens[1]) > 0, out, 0.0)
    for k in range(slots):
        mixer[k] = out[k * steps : (k + 1) * steps].astype(BF16)


def local(
    hidden_pre,
    coeff_pre,
    gate_pre,
    step_raw,
    cache_rows,
    lengths,
    owners,
    page_table,
    conv_hidden,
    conv_coeff,
    step_bias,
    decay_log,
    skip_gain,
    norm_gain,
    new_hidden,
    new_coeff,
    new_gate,
    new_step,
    new_query,
    new_cache,
):
    devices = lax.axis_size(AXES)
    prompts, span, columns = hidden_pre.shape
    slots = new_hidden.shape[0]
    local_heads = step_raw.shape[0]
    cache_width = cache_rows.shape[2]
    kept_rows = slots * cache_rows.shape[1] * cache_width // LANES
    per_owner = pltpu.SMEM((devices,), jnp.int32)
    per_prompt = pltpu.SMEM((prompts,), jnp.int32)

    owners = owners[:, 0]
    send = pl.pallas_call(
        pack_kernel,
        out_shape=jax.ShapeDtypeStruct((devices, span + NEW, LANES), BF16),
        in_specs=[ANY, ANY, ANY, ANY],
        out_specs=VMEM,
        scratch_shapes=[
            pltpu.VMEM(new_hidden.shape, BF16),
            pltpu.VMEM(new_coeff.shape, BF16),
            pltpu.VMEM(new_step.shape, F32),
            pltpu.SemaphoreType.DMA((3 + devices,)),
        ],
        name="pack",
    )(coeff_pre, new_hidden, new_coeff, new_step)
    recv = lax.all_to_all(send, AXES, split_axis=0, concat_axis=0, tiled=True)
    chips = devices // 2
    kept = pl.pallas_call(
        pack_cache_kernel,
        out_shape=(jax.ShapeDtypeStruct((2, kept_rows, LANES), BF16),) * chips,
        in_specs=[SMEM, VMEM],
        out_specs=(VMEM,) * chips,
        scratch_shapes=[per_owner, pltpu.SMEM((devices * slots,), jnp.int32)],
        compiler_params=PARAMS,
        cost_estimate=cost(3),
        name="pack_cache",
    )(owners, cache_rows)
    kept = list(kept)
    first = (1, 3, 6, 7, 5, 4, 2)
    for m in (*first, *range(len(first) + 1, chips)):
        kept[m] = lax.ppermute(kept[m], "tensor", [(i, i ^ m) for i in range(chips)])
    before = pl.pallas_call(
        before_kernel,
        out_shape=(
            jax.ShapeDtypeStruct((prompts, span, columns), BF16),
            jax.ShapeDtypeStruct((CONVK - 1, prompts, columns), F32),
            jax.ShapeDtypeStruct((8, columns), F32),
            jax.ShapeDtypeStruct((local_heads, prompts, LANES), F32),
            jax.ShapeDtypeStruct((local_heads, prompts, LANES), F32),
        ),
        in_specs=[SMEM] * 4 + [VMEM] * 3,
        out_specs=(VMEM,) * 5,
        compiler_params=PARAMS,
        cost_estimate=cost(4),
        name="before",
    )(lengths, step_bias, decay_log, skip_gain, conv_hidden, hidden_pre, step_raw)
    early = (1, 3, 6)
    recv, sums, *held = lax.optimization_barrier(
        (recv, before[-1], *(kept[m] for m in early))
    )
    before = (*before[:-1], sums)
    for m, block in zip(early, held):
        kept[m] = block

    mine = pl.pallas_call(
        coeff_kernel,
        grid=(1,),
        out_shape=jax.ShapeDtypeStruct((prompts, ROWS, LANES), BF16),
        in_specs=[
            SMEM,
            SMEM,
            VMEM,
            pl.BlockSpec((devices, span + NEW, LANES), lambda i: (0, 0, 0)),
        ],
        out_specs=VMEM,
        scratch_shapes=[per_owner, per_prompt],
        compiler_params=PARAMS,
        cost_estimate=cost(2),
        name="coeff",
    )(owners, lengths, conv_coeff, recv)
    other = lax.ppermute(mine, "side", [(0, 1), (1, 0)])

    new_block = span // NEW
    gated, fin = pl.pallas_call(
        main_kernel,
        grid=(1,),
        out_shape=(
            jax.ShapeDtypeStruct((prompts, span, columns), F32),
            jax.ShapeDtypeStruct((devices, prompts + 8, LANES), BF16),
        ),
        in_specs=[SMEM] * 2
        + [VMEM] * 3
        + [pl.BlockSpec((devices, NEW, LANES), lambda i: (0, new_block, 0))]
        + [VMEM] * 6,
        out_specs=(VMEM, VMEM),
        scratch_shapes=[
            pltpu.VMEM((devices, 8, LANES), F32),
            per_owner,
            per_prompt,
            pltpu.VMEM((2, prompts, LANES), F32),
            pltpu.VMEM((2, prompts, columns), F32),
            pltpu.VMEM((prompts, 8, LANES), F32),
            pltpu.VMEM((prompts, 8, LANES), F32),
        ],
        compiler_params=PARAMS,
        cost_estimate=cost(10),
        name="main",
    )(
        owners,
        lengths,
        conv_hidden,
        mine,
        other,
        recv,
        gate_pre,
        *before,
    )
    fin, *kept = lax.optimization_barrier((fin, *kept))
    crossed = pl.pallas_call(
        stack_kernel,
        out_shape=jax.ShapeDtypeStruct((chips, kept_rows, LANES), BF16),
        in_specs=[VMEM] * chips,
        out_specs=VMEM,
        compiler_params=PARAMS,
        cost_estimate=cost(1),
        name="stack",
    )(*kept)
    crossed = lax.ppermute(crossed, "side", [(0, 1), (1, 0)])
    fin_got = lax.all_to_all(fin, AXES, split_axis=0, concat_axis=0, tiled=True)

    cache_pool, decode_attention = pl.pallas_call(
        cache_kernel,
        out_shape=(
            jax.ShapeDtypeStruct((page_table.shape[1], BLK, cache_width), BF16),
            jax.ShapeDtypeStruct(new_query.shape, BF16),
        ),
        in_specs=[SMEM] * 3 + [VMEM] * (3 + chips),
        out_specs=(VMEM, VMEM),
        scratch_shapes=[pltpu.VMEM((slots * span, cache_width), BF16)],
        compiler_params=PARAMS,
        cost_estimate=cost(5),
        name="cache",
    )(owners, lengths, page_table, new_query, new_cache, crossed, *kept)

    fin_got, cache_pool = lax.optimization_barrier((fin_got, cache_pool))
    prefill_out, decode_mixer = pl.pallas_call(
        final_kernel,
        out_shape=(
            jax.ShapeDtypeStruct(hidden_pre.shape, BF16),
            jax.ShapeDtypeStruct(new_gate.shape, BF16),
        ),
        in_specs=[SMEM, SMEM, VMEM, VMEM, VMEM, VMEM],
        out_specs=(VMEM, VMEM),
        compiler_params=PARAMS,
        name="final",
    )(owners, lengths, norm_gain.reshape(1, -1), fin_got, gated, new_gate)
    return (prefill_out, cache_pool, decode_mixer, decode_attention)


def solution(mesh):
    own = P(("group", "tensor", "side"), None, None)
    placed = (
        P("group", None, ("tensor", "side")),
        own,
        P("group", None, ("tensor", "side")),
        P(("tensor", "side"), "group", None),
        P("group", ("tensor", "side"), None),
        P("group"),
        P("group", None),
        P(("group", "tensor", "side"), None),
        P(),
        P(),
        P(),
        P(),
        P(),
        P(),
        own,
        own,
        own,
        own,
        own,
        own,
    )
    return jax.shard_map(
        local,
        mesh=mesh,
        in_specs=placed,
        out_specs=(P("group", None, ("tensor", "side")), own, own, own),
        check_vma=False,
    )
```
